128 devices in a mesh: cell: 32 (over y, z, core), wall: 4 (over x).
Axes of the slice: x: 4, y: 4, z: 4, core: 2. Of those that a mesh axis runs over, the one named last changes fastest.
Arguments:
- cell_points: float32 [1024, 3, 544], P('cell'), may hold values from -4 to 4
- cell_density: float32 [1024, 3, 544], P('cell'), may hold values from -6 to 6
- cell_weights: float32 [1024, 544], P('cell'), may hold values from 0.1 to 1
- near_device: int32 [1024, 8], P('cell'), may hold values from 0 to 31, all different within a row; in each aligned block of 32 rows (0 to 31, 32 to 63, ...) at most 16 rows name the same one
- near_slot: int32 [1024, 8], P('cell'), may hold values from 0 to 31
- near_wall: int32 [1024, 8], P('cell'), may hold values from 0 to 255
- wall_points: float32 [8192, 3, 256], P(('cell', 'wall')), may hold values from -4 to 4
- wall_density: float32 [8192, 3, 256], P(('cell', 'wall')), may hold values from -6 to 6
- wall_weights: float32 [8192, 256], P(('cell', 'wall')), may hold values from 0.1 to 1
Outputs:
- cell_velocity: float32 [1024, 3, 544], P('cell', None, 'wall')
- wall_velocity: float32 [8192, 3, 256], P(('cell', 'wall'))
The draws below stay inside these ranges and needn't reach their ends.
Inputs may be any that keep to these rules, and one draw needn't show every extreme that they name: `near_device`: the 8 entries of a row are distinct. Among the rows of one index of cell (32 rows) no value is named more than 16 times, a bound that some block reaches.
All inputs are finite; a program needn't handle non-finite values.
Results may differ from the reference program's by a relative error of at most 0.00005.
Values sent between devices are 32-bit elements; how exact they have to be, the bound alone decides.
A program may use at most 128 MiB of HBM per device.

```python
import math
import jax
import jax.numpy as jnp
import numpy as np
from jax import lax

P_SIZE = 544
PW = 256
NEAR = 8
NW = 8
CELL_DEV = 32
CAP = 16
CELLS = 1024
PATCH_GROUP = 256
PATCHES = 8192
N_CELL = 32


def touch_ends(entries, rng, least, high):
    longest = entries.shape.index(max(entries.shape))
    spots = []
    for shift in (0, 1):
        where = [jax.random.randint(jax.random.fold_in(rng, axis), (), 0, length) for axis, length in enumerate(entries.shape)]
        where[longest] = (where[longest] + shift) % entries.shape[longest]
        spots.append(tuple(where))
    return entries.at[spots[0]].set(least).at[spots[1]].set(high)


def levels(stream_key, extent, cuts, smallest, high):
    def one(position, blocks):
        draws = jax.random.uniform(jax.random.fold_in(jax.random.fold_in(stream_key, 6), position), (blocks,), jnp.float32, smallest / len(cuts), high / len(cuts))
        return jnp.repeat(jnp.exp(draws), extent[position] // blocks).reshape((-1,) + (1,) * (len(extent) - position - 1))

    gain = one(*cuts[0])
    for cut in cuts[1:]:
        gain = gain * one(*cut)
    return gain


def assign_block(rng, own, number, rows, amount, top, bound, lean):
    ranking = jax.random.permutation(rng, amount)
    crowded, usual = portions_of(amount, rows * top, bound, lean, True), portions_of(amount, rows * top, bound, lean, False)
    places = jnp.arange(amount)

    def named(lengths, offset_by):
        used = int((lengths > 0).sum())
        fixed = max(1, used // 4)
        moved = fixed + (places - fixed + offset_by * (used - fixed)) % max(1, amount - fixed)
        return jnp.zeros((amount,), jnp.int32).at[ranking[jnp.where(places < fixed, places, moved)]].set(jnp.asarray(lengths, jnp.int32))

    lengths = jnp.where(number % 4 == 0, named(crowded, number // 4), named(usual, number - number // 4 - 1))
    mixed = jax.random.permutation(jax.random.fold_in(own, 3), amount)
    donor, taker = mixed[0:amount // 2 * 2:2], mixed[1:amount // 2 * 2:2]
    margin = jnp.minimum(lengths[donor] - 1, bound - lengths[taker]) // 2
    margin = jnp.where((donor == ranking[0]) | (taker == ranking[0]) | (lengths[taker] == 0), 0, jnp.maximum(margin, 0))
    moved = jax.random.randint(jax.random.fold_in(own, 4), (amount // 2,), 0, 1 << 20) % (margin + 1)
    lengths = lengths.at[donor].add(-moved).at[taker].add(moved)
    items = jnp.searchsorted(jnp.cumsum(lengths), jnp.arange(rows * top), side="right").astype(jnp.int32)
    table = items.reshape(top, rows).T
    table = table[jax.random.permutation(jax.random.fold_in(own, 1), rows)]
    offset_by = jax.random.randint(jax.random.fold_in(own, 2), (rows, 1), 0, top)
    return jnp.take_along_axis(table, (jnp.arange(top)[None, :] + offset_by) % top, axis=1)


def portions_of(amount, total, reach, lean, full):
    loads = [(1 << 20) // math.isqrt(grade ** lean) + 1 for grade in range(1, amount + 1)]
    largest = reach if full else min(reach, max(-(-total // amount), total * loads[0] // sum(loads)))
    least = 1 if total - largest >= amount - 1 else 0
    given, surplus = [largest] + [least] * (amount - 1), total - largest - least * (amount - 1)
    while surplus > 0:
        movable = [i for i in range(1, amount) if given[i] < largest] or [i for i in range(1, amount) if given[i] < reach]
        whole, remaining = sum([loads[i] for i in movable]), surplus
        for i in movable:
            addition = min(reach - given[i], max(1, remaining * loads[i] // whole), surplus)
            given[i] = given[i] + addition
            surplus = surplus - addition
    return np.array(given)


def scatter_about(own_key, shape, deviation, limit, shards=(), held_as=jnp.bfloat16):
    factor_of = levels(own_key, shape, shards, -0.22, 0.18) if shards else 1.0
    drawn = jax.random.normal(own_key, shape, jnp.float32) * deviation * factor_of
    return jnp.minimum(jnp.maximum(drawn, -limit), limit).astype(held_as)


def setup_inputs(seed: int = 0) -> dict:
    key_list = jax.random.split(jax.random.key(seed), 10)
    cell_points = jnp.clip(jax.random.uniform(key_list[0], (CELLS, 3, P_SIZE), jnp.float32, -4.0, 4.0) * levels(key_list[0], (CELLS, 3, P_SIZE), ((0, 32),), -0.4, 0.0), -4.0, 4.0)
    cell_density = scatter_about(key_list[1], (CELLS, 3, P_SIZE), 1.0, 6.0, ((0, 32),), jnp.float32)
    cell_weights = jnp.clip(jnp.exp(math.log(1.0) - 2.3025851 * jax.random.uniform(key_list[2], (CELLS, P_SIZE), jnp.float32) ** levels(key_list[2], (CELLS, P_SIZE), ((0, 32),), -0.2, 0.2)), 0.1, 1.0)
    near_device_keys = jax.random.split(jax.random.fold_in(key_list[3], 1), CELLS // CELL_DEV)
    near_device_turns = jax.random.permutation(jax.random.fold_in(key_list[3], 3), CELLS // CELL_DEV)
    near_device = jax.vmap(lambda own, number: assign_block(jax.random.fold_in(key_list[3], 2), own, number, CELL_DEV, N_CELL, NEAR, CAP, 2))(near_device_keys, near_device_turns).reshape((CELLS, NEAR))
    near_slot = touch_ends(jax.random.randint(key_list[4], (CELLS, NEAR), 0, CELL_DEV), jax.random.fold_in(key_list[4], 1), 0, CELL_DEV - 1).astype(jnp.int32)
    near_wall = touch_ends(jax.random.randint(key_list[5], (CELLS, NW), 0, PATCH_GROUP), jax.random.fold_in(key_list[5], 1), 0, PATCH_GROUP - 1).astype(jnp.int32)
    wall_points = jnp.clip(jax.random.uniform(key_list[6], (PATCHES, 3, PW), jnp.float32, -4.0, 4.0) * levels(key_list[6], (PATCHES, 3, PW), ((0, 128),), -0.4, 0.0), -4.0, 4.0)
    wall_density = scatter_about(key_list[7], (PATCHES, 3, PW), 1.0, 6.0, ((0, 128),), jnp.float32)
    wall_weights = jnp.clip(jnp.exp(math.log(1.0) - 2.3025851 * jax.random.uniform(key_list[8], (PATCHES, PW), jnp.float32) ** levels(key_list[8], (PATCHES, PW), ((0, 128),), -0.2, 0.2)), 0.1, 1.0)
    return {"cell_points": cell_points, "cell_density": cell_density, "cell_weights": cell_weights, "near_device": near_device, "near_slot": near_slot, "near_wall": near_wall, "wall_points": wall_points, "wall_density": wall_density, "wall_weights": wall_weights}


blob_square = 0.25
stokes_factor = 0.039788735772973836

def stokeslet(targets, sources, force, weight):
    gap = targets[:, :, None] - sources[:, None, :]
    dist = lax.optimization_barrier(jnp.sum(gap * gap, axis=0))
    shifted = dist + blob_square
    inverse = 1.0 / (shifted * jnp.sqrt(shifted))
    loaded = force * weight[None, :]
    along = lax.optimization_barrier(jnp.sum(gap * loaded[:, None, :], axis=0))
    first = lax.optimization_barrier(jnp.sum(loaded[:, None, :] * ((dist + 2.0 * blob_square) * inverse)[None], axis=2))
    second = lax.optimization_barrier(jnp.sum(gap * (along * inverse)[None], axis=2))
    return stokes_factor * (first + second)

def reference(cell_points, cell_density, cell_weights, near_device, near_slot, near_wall, wall_points, wall_density, wall_weights):
    near_ids = (near_device * CELL_DEV + near_slot).astype(jnp.int32)
    owners = (jnp.arange(CELLS, dtype=jnp.int32) // CELL_DEV).astype(jnp.int32)
    patch_ids = (owners[:, None] * PATCH_GROUP + near_wall).astype(jnp.int32)

    def per_cell(items):
        points, density, neighbours, patches = items
        src_points = cell_points[neighbours].transpose(1, 0, 2).reshape(3, NEAR * P_SIZE)
        src_density = cell_density[neighbours].transpose(1, 0, 2).reshape(3, NEAR * P_SIZE)
        src_weights = cell_weights[neighbours].reshape(NEAR * P_SIZE)
        near_part = stokeslet(points, src_points, src_density, src_weights)
        wpts = wall_points[patches].transpose(1, 0, 2).reshape(3, NW * PW)
        wden = wall_density[patches].transpose(1, 0, 2).reshape(3, NW * PW)
        wwts = wall_weights[patches].reshape(NW * PW)
        wall_part = stokeslet(points, wpts, wden, wwts)
        return 0.5 * density + near_part + wall_part

    def per_wall(items):
        points, density, weights, patches = items
        wpts = wall_points[patches].transpose(1, 0, 2).reshape(3, NW * PW)
        back = stokeslet(wpts, points, density, weights)
        return back.reshape(3, NW, PW).transpose(1, 0, 2)
    cell_velocity = lax.map(per_cell, (cell_points, cell_density, near_ids, patch_ids))
    to_wall = lax.map(per_wall, (cell_points, cell_density, cell_weights, patch_ids))
    summed = jax.ops.segment_sum(to_wall.reshape(CELLS * NW, 3, PW), patch_ids.reshape(CELLS * NW), num_segments=PATCHES)
    wall_velocity = 0.5 * wall_density + summed
    return (cell_velocity, wall_velocity)
```

```python
import jax
import jax.numpy as jnp
from jax import lax
from jax.experimental import pallas as pl
from jax.experimental.pallas import tpu as pltpu
from jax.sharding import PartitionSpec as P

f32 = jnp.float32
bf16 = jnp.bfloat16
two_stokes_factor = 2.0 * 0.039788735772973836
levels = ((1, 1), (1, 2), (1, 3), (2, 1), (2, 2), (3, 1))
depth = 64
lanes = 128


def split3(x):
    first = x.astype(bf16).astype(f32)
    rest = x - first
    second = rest.astype(bf16).astype(f32)
    return first, second, rest - second


def rounded3(x):
    first = lax.reduce_precision(x, 8, 7)
    rest = x - first
    second = lax.reduce_precision(rest, 8, 7)
    return first, second, rest - second


def source_features(raw):
    y = [raw[i : i + 1, :] for i in range(3)]
    g = [raw[i : i + 1, :] for i in range(3, 6)]
    square = y[0] * y[0] + y[1] * y[1] + y[2] * y[2] + 1.0
    dot = g[0] * y[0] + g[1] * y[1] + g[2] * y[2]
    rows = jnp.concatenate(
        [-2.0 * y[0], -2.0 * y[1], -2.0 * y[2], square, g[0], g[1], g[2], -dot], axis=0
    )
    parts = split3(rows)
    one = jnp.ones_like(rows)
    stack = [parts[p - 1] for p, _ in levels] + [one, jnp.zeros_like(rows)]
    return jnp.concatenate(stack, axis=0).astype(bf16)


def target_features(x, load):
    xs, ls = rounded3(x), rounded3(load)
    square = rounded3(jnp.sum(x * x, axis=1, keepdims=True))
    dot = rounded3(jnp.sum(x * load, axis=1, keepdims=True))
    zero, one = jnp.zeros_like(square[0]), jnp.ones_like(square[0])
    zero4 = jnp.concatenate([zero] * 4, axis=1)
    dist, along, back = [], [], []
    for _, q in levels:
        unit = one if q == 1 else zero
        dist += [xs[q - 1], unit, zero4]
        along += [zero4, xs[q - 1], unit]
        back += [-0.5 * ls[q - 1], zero, zero4]
    dist += list(square) + [zero] * 5 + [zero4] * 2
    along += [zero4] * 4
    back += [-d for d in dot] + [zero] * 5 + [zero4] * 2
    kinds = [jnp.swapaxes(jnp.concatenate(k, axis=1), 1, 2) for k in (dist, along, back)]
    return jnp.concatenate(kinds, axis=1).astype(bf16)


def products(a_ref, j, rows, w_ref, s_ref):
    n = w_ref.shape[1]
    for c in range(0, n, 256):
        e = min(n, c + 256)
        s_ref[:, c:e] = jnp.dot(a_ref[j, :rows], w_ref[:, c:e], preferred_element_type=f32)


def source_rows(r_ref, cols):
    return [jnp.broadcast_to(r_ref[i : i + 1, cols], (8, lanes)) for i in range(6)]


def added(total, term):
    return term if total is None else total + term


def near_kernel(
    ids_ref, gathered_ref, center_ref, target_ref, point_ref, wall_ref, out_ref, s0, s1, r0, r1, w0, w1, sums
):
    cells = out_ref.shape[0]
    points = out_ref.shape[2]
    tiles = r0.shape[1] // lanes

    def prepare(j, r_ref, w_ref):
        center = center_ref[j]
        lane = lax.broadcasted_iota(jnp.int32, (8, lanes), 1)
        tail = jnp.zeros((8, lanes), f32)
        parts = []
        for k in range(8):
            block = gathered_ref[ids_ref[j, k]]
            parts.append(block - center)
            last = jnp.broadcast_to(block[6:7, :], (8, lanes))
            last = pltpu.roll(last, 8 * k, 1, stride=8, stride_axis=0)
            tail = jnp.where((lane >= 8 * k) & (lane < 8 * k + 8), last, tail)
        parts.append(jnp.where(lane < 64, tail - center, 0.0))
        raw = jnp.concatenate(parts, axis=1)
        r_ref[...] = raw
        w_ref[...] = source_features(raw)

    def evaluate(j, s_ref, r_ref):
        blocks = 4
        for start in range(0, points, 8 * blocks):
            acc = [[None] * blocks for _ in range(4)]
            for c in range(tiles):
                cols = slice(c * lanes, c * lanes + lanes)
                src = source_rows(r_ref, cols)
                for b in range(blocks):
                    top = start + 8 * b
                    h = lax.rsqrt(s_ref[top : top + 8, cols])
                    cube = h * h * h
                    whole = h + cube
                    m = s_ref[points + top : points + top + 8, cols] * cube
                    acc[3][b] = added(acc[3][b], m)
                    for k in range(3):
                        acc[k][b] = added(acc[k][b], whole * src[3 + k]) - m * src[k]
            for b in range(blocks):
                top = start + 8 * b
                for k in range(4):
                    sums[top : top + 8, k : k + 1] = jnp.sum(acc[k][b], axis=1, keepdims=True)
        flat = sums[...].T[0:8, :points]
        out_ref[j] = flat + point_ref[j] * flat[3:4, :] + wall_ref[j]

    def step(j, s_ref, r_ref, w_ref):
        prepare(j, r_ref, w_ref)
        products(target_ref, j, 2 * points, w_ref, s_ref)

    step(0, s0, r0, w0)

    def body(i, carry):
        j = 2 * i
        step(j + 1, s1, r1, w1)
        evaluate(j, s0, r0)
        step(jnp.minimum(j + 2, cells - 1), s0, r0, w0)
        evaluate(j + 1, s1, r1)
        return carry

    lax.fori_loop(0, cells // 2, body, 0)


def wall_kernel(
    ids_ref, patch_ref, center_ref, target_ref, point_ref, column_ref, out_ref, back_ref, s0, s1, r0, r1, w0, w1, sums
):
    cells = out_ref.shape[0]
    points = out_ref.shape[2]
    tiles = r0.shape[1] // lanes
    lane = lax.broadcasted_iota(jnp.int32, (8, lanes), 1)
    back_ref[...] = jnp.zeros_like(back_ref)

    def prepare(j, r_ref, w_ref):
        center = center_ref[j]
        parts = []
        for t in range(tiles):
            left, right = ids_ref[j, 2 * t], ids_ref[j, 2 * t + 1]
            one = pltpu.roll(patch_ref[left // 2], 64 * (left % 2), 1)
            two = pltpu.roll(patch_ref[right // 2], 64 * (1 - right % 2), 1)
            parts.append(jnp.where(lane < 64, one, two) - center)
        raw = jnp.concatenate(parts, axis=1)
        r_ref[...] = raw
        w_ref[...] = source_features(raw)

    def evaluate(j, s_ref, r_ref):
        blocks = 2
        back = [[None] * 4 for _ in range(tiles)]
        for start in range(0, points, 8 * blocks):
            acc = [[None] * blocks for _ in range(4)]
            own = [
                [
                    jnp.broadcast_to(column_ref[j, start + 8 * b : start + 8 * b + 8, k : k + 1], (8, lanes))
                    for k in range(6)
                ]
                for b in range(blocks)
            ]
            for c in range(tiles):
                cols = slice(c * lanes, c * lanes + lanes)
                src = source_rows(r_ref, cols)
                for b in range(blocks):
                    top = start + 8 * b
                    h = lax.rsqrt(s_ref[top : top + 8, cols])
                    cube = h * h * h
                    whole = h + cube
                    m = s_ref[points + top : points + top + 8, cols] * cube
                    n = s_ref[2 * points + top : 2 * points + top + 8, cols] * cube
                    acc[3][b] = added(acc[3][b], m)
                    back[c][3] = added(back[c][3], n)
                    for k in range(3):
                        acc[k][b] = added(acc[k][b], whole * src[3 + k]) - m * src[k]
                        back[c][k] = added(back[c][k], whole * own[b][3 + k]) - n * own[b][k]
            for b in range(blocks):
                top = start + 8 * b
                for k in range(4):
                    sums[top : top + 8, k : k + 1] = jnp.sum(acc[k][b], axis=1, keepdims=True)
        flat = sums[...].T[0:8, :points]
        out_ref[j] = flat + point_ref[j] * flat[3:4, :]
        for c in range(tiles):
            rows = [jnp.sum(back[c][k], axis=0, keepdims=True) for k in range(4)]
            rows = jnp.concatenate(rows + [jnp.zeros((4, lanes), f32)], axis=0)
            term = rows + r_ref[:, c * lanes : c * lanes + lanes] * rows[3:4, :]
            for half in range(2):
                patch = ids_ref[j, 2 * c + half]
                odd = patch % 2
                moved = pltpu.roll(term, 64 * (odd if half == 0 else 1 - odd), 1)
                kept = jnp.where((lane >= 64) == (odd == 1), moved, 0.0)
                back_ref[patch // 2] += kept

    def step(j, s_ref, r_ref, w_ref):
        prepare(j, r_ref, w_ref)
        products(target_ref, j, 3 * points, w_ref, s_ref)

    step(0, s0, r0, w0)

    def body(i, carry):
        j = 2 * i
        step(j + 1, s1, r1, w1)
        evaluate(j, s0, r0)
        step(jnp.minimum(j + 2, cells - 1), s0, r0, w0)
        evaluate(j + 1, s1, r1)
        return carry

    lax.fori_loop(0, cells // 2, body, 0)


def scratch(points, kinds, tiles):
    return [
        pltpu.VMEM((kinds * points, tiles * lanes), f32),
        pltpu.VMEM((kinds * points, tiles * lanes), f32),
        pltpu.VMEM((8, tiles * lanes), f32),
        pltpu.VMEM((8, tiles * lanes), f32),
        pltpu.VMEM((depth, tiles * lanes), bf16),
        pltpu.VMEM((depth, tiles * lanes), bf16),
        pltpu.VMEM((-(-points // lanes) * lanes, lanes), f32),
    ]


def local(
    cell_points,
    cell_density,
    cell_weights,
    near_device,
    near_slot,
    near_wall,
    wall_points,
    wall_density,
    wall_weights,
):
    wall_count = lax.axis_size("wall")
    wall_index = lax.axis_index("wall")
    cells, _, points = cell_points.shape
    patch_dev, _, patch_pts = wall_points.shape
    quarter = points // wall_count
    extra = quarter - lanes
    part = patch_pts // wall_count
    vmem = pl.BlockSpec(memory_space=pltpu.VMEM)
    smem = pl.BlockSpec(memory_space=pltpu.SMEM)
    params = pltpu.CompilerParams(vmem_limit_bytes=60 * 2**20)

    cell_load = cell_density * cell_weights[:, None, :]
    raw = jnp.concatenate([2.0 * cell_points, cell_load], axis=1)
    mine = lax.dynamic_slice_in_dim(raw, wall_index * quarter, quarter, 2)
    tail = jnp.zeros((cells, 1, lanes), f32)
    for q in range(6):
        at = (lanes - extra * q) % lanes
        tail = tail.at[:, 0, at : at + extra].set(mine[:, q, lanes:])
    block = jnp.concatenate([mine[:, :, :lanes], tail, jnp.zeros((cells, 1, lanes), f32)], axis=1)
    gathered = lax.all_gather(block, "cell", axis=0, tiled=True)

    wall_raw = jnp.concatenate(
        [2.0 * wall_points, wall_density * wall_weights[:, None, :], jnp.zeros((patch_dev, 2, patch_pts), f32)],
        axis=1,
    )
    wall_raw = wall_raw.reshape(patch_dev // 2, 2, 8, wall_count, part).transpose(3, 0, 2, 1, 4)
    wall_raw = wall_raw.reshape(wall_count * (patch_dev // 2), 8, 2 * part)
    patches = lax.all_to_all(wall_raw, "wall", split_axis=0, concat_axis=0, tiled=True)

    center = jnp.mean(cell_points, axis=2, keepdims=True)
    point = 2.0 * cell_points - 2.0 * center
    center_block = jnp.concatenate([2.0 * center, jnp.zeros((cells, 5, 1), f32)], axis=1)
    center_block = jnp.broadcast_to(center_block, (cells, 8, lanes))
    point_block = jnp.concatenate([point, jnp.zeros((cells, 5, points), f32)], axis=1)
    column = jnp.swapaxes(jnp.concatenate([point, cell_load], axis=1), 1, 2)
    target = target_features(point, cell_load)

    tiles = near_wall.shape[1] * part // lanes
    wall_term, back = pl.pallas_call(
        wall_kernel,
        out_shape=(
            jax.ShapeDtypeStruct((cells, 8, points), f32),
            jax.ShapeDtypeStruct(patches.shape, f32),
        ),
        in_specs=[smem] + [vmem] * 5,
        out_specs=(vmem, vmem),
        scratch_shapes=scratch(points, 3, tiles),
        compiler_params=params,
        cost_estimate=pl.CostEstimate(flops=10**9, bytes_accessed=10**8, transcendentals=0),
        name="wall_pairs",
    )(near_wall, patches, center_block, target, point_block, column)

    near_ids = near_device * cells + near_slot
    tiles = near_device.shape[1] + 1
    total = pl.pallas_call(
        near_kernel,
        out_shape=jax.ShapeDtypeStruct((cells, 8, points), f32),
        in_specs=[smem] + [vmem] * 5,
        out_specs=vmem,
        scratch_shapes=scratch(points, 2, tiles),
        compiler_params=params,
        cost_estimate=pl.CostEstimate(flops=10**9, bytes_accessed=10**8, transcendentals=0),
        name="near_pairs",
    )(near_ids, gathered, center_block, target, point_block, wall_term)

    share = lax.psum_scatter(total[:, :3, :], "wall", scatter_dimension=2, tiled=True)
    own = lax.dynamic_slice_in_dim(cell_density, wall_index * quarter, quarter, 2)
    velocity = 0.5 * own + two_stokes_factor * share

    back = lax.all_to_all(back[:, :3, :], "wall", split_axis=0, concat_axis=0, tiled=True)
    back = back.reshape(wall_count, patch_dev // 2, 3, 2, part).transpose(1, 3, 2, 0, 4)
    wall_velocity = 0.5 * wall_density + two_stokes_factor * back.reshape(patch_dev, 3, patch_pts)
    return (velocity, wall_velocity)


def solution(mesh):
    in_specs = (
        P("cell", None, None),
        P("cell", None, None),
        P("cell", None),
        P("cell", None),
        P("cell", None),
        P("cell", None),
        P(("cell", "wall"), None, None),
        P(("cell", "wall"), None, None),
        P(("cell", "wall"), None),
    )
    out_specs = (P("cell", None, "wall"), P(("cell", "wall"), None, None))
    return jax.shard_map(local, mesh=mesh, in_specs=in_specs, out_specs=out_specs, check_vma=False)
```

```python
import jax
import jax.numpy as jnp
from jax import lax
from jax.experimental import pallas as pl
from jax.experimental.pallas import tpu as pltpu
from jax.sharding import PartitionSpec as P

f32 = jnp.float32
bf16 = jnp.bfloat16
two_stokes_factor = 2.0 * 0.039788735772973836
levels = ((1, 1), (1, 2), (1, 3), (2, 1), (2, 2), (3, 1))
depth = 64
lanes = 128


def split3(x):
    first = x.astype(bf16).astype(f32)
    rest = x - first
    second = rest.astype(bf16).astype(f32)
    return first, second, rest - second


def source_features(raw):
    y = [raw[i : i + 1, :] for i in range(3)]
    g = [raw[i : i + 1, :] for i in range(3, 6)]
    square = y[0] * y[0] + y[1] * y[1] + y[2] * y[2] + 1.0
    dot = g[0] * y[0] + g[1] * y[1] + g[2] * y[2]
    rows = jnp.concatenate(
        [-2.0 * y[0], -2.0 * y[1], -2.0 * y[2], square, g[0], g[1], g[2], -dot], axis=0
    )
    parts = split3(rows)
    one = jnp.ones_like(rows)
    stack = [parts[p - 1] for p, _ in levels] + [one, jnp.zeros_like(rows)]
    return jnp.concatenate(stack, axis=0).astype(bf16)


def prepare_own(j, point_ref, density_ref, weight_ref, feature_ref, own_ref, a_ref, kinds):
    points = point_ref.shape[2]
    x = 2.0 * point_ref[j]
    center = jnp.sum(x, axis=1, keepdims=True) * (1.0 / points)
    x = x - center
    load = density_ref[j] * weight_ref[pl.ds(j, 1), :]
    own_ref[0:3, :points] = x
    own_ref[3:6, :points] = load
    xs = split3(x)
    squares = split3(jnp.sum(x * x, axis=0, keepdims=True))
    for i, (_, q) in enumerate(levels):
        feature_ref[8 * i : 8 * i + 3, :points] = xs[q - 1]
        feature_ref[depth + 8 * i + 4 : depth + 8 * i + 7, :points] = xs[q - 1]
    for i in range(3):
        feature_ref[48 + i : 49 + i, :points] = squares[i]
    if kinds == 3:
        ls = split3(-0.5 * load)
        dots = split3(-jnp.sum(x * load, axis=0, keepdims=True))
        for i, (_, q) in enumerate(levels):
            feature_ref[2 * depth + 8 * i : 2 * depth + 8 * i + 3, :points] = ls[q - 1]
        for i in range(3):
            feature_ref[2 * depth + 48 + i : 2 * depth + 49 + i, :points] = dots[i]
    for kind in range(kinds):
        turned = feature_ref[kind * depth : kind * depth + depth, :].T
        a_ref[kind * points : kind * points + points, :] = turned[:points].astype(bf16)
    return jnp.concatenate([jnp.broadcast_to(center, (3, lanes)), jnp.zeros((5, lanes), f32)], axis=0)


def start_features(feature_ref):
    feature_ref[...] = jnp.zeros_like(feature_ref)
    one = jnp.ones((1, feature_ref.shape[1]), f32)
    for i, (_, q) in enumerate(levels):
        if q == 1:
            feature_ref[8 * i + 3 : 8 * i + 4, :] = one
            feature_ref[depth + 8 * i + 7 : depth + 8 * i + 8, :] = one


def products(a_ref, w_ref, s_ref):
    n = w_ref.shape[1]
    for c in range(0, n, 256):
        e = min(n, c + 256)
        s_ref[:, c:e] = jnp.dot(a_ref[...], w_ref[:, c:e], preferred_element_type=f32)


def source_rows(r_ref, cols):
    return [jnp.broadcast_to(r_ref[i : i + 1, cols], (8, lanes)) for i in range(6)]


def added(total, term):
    return term if total is None else total + term


def near_kernel(
    ids_ref,
    gathered_ref,
    point_ref,
    density_ref,
    weight_ref,
    wall_ref,
    out_ref,
    s0,
    s1,
    r0,
    r1,
    w0,
    w1,
    o0,
    o1,
    a0,
    a1,
    feature_ref,
    sums,
):
    cells = out_ref.shape[0]
    points = out_ref.shape[2]
    tiles = r0.shape[1] // lanes

    def prepare(j, center, r_ref, w_ref):
        lane = lax.broadcasted_iota(jnp.int32, (8, lanes), 1)
        tail = jnp.zeros((8, lanes), f32)
        parts = []
        for k in range(8):
            block = gathered_ref[ids_ref[j, k]]
            parts.append(block - center)
            last = jnp.broadcast_to(block[6:7, :], (8, lanes))
            last = pltpu.roll(last, 8 * k, 1, stride=8, stride_axis=0)
            tail = jnp.where((lane >= 8 * k) & (lane < 8 * k + 8), last, tail)
        parts.append(jnp.where(lane < 64, tail - center, 0.0))
        raw = jnp.concatenate(parts, axis=1)
        r_ref[...] = raw
        w_ref[...] = source_features(raw)

    def evaluate(j, s_ref, r_ref, own_ref):
        blocks = 4
        for start in range(0, points, 8 * blocks):
            acc = [[None] * blocks for _ in range(4)]
            for c in range(tiles):
                cols = slice(c * lanes, c * lanes + lanes)
                src = source_rows(r_ref, cols)
                for b in range(blocks):
                    top = start + 8 * b
                    h = lax.rsqrt(s_ref[top : top + 8, cols])
                    cube = h * h * h
                    whole = h + cube
                    m = s_ref[points + top : points + top + 8, cols] * cube
                    acc[3][b] = added(acc[3][b], m)
                    for k in range(3):
                        acc[k][b] = added(acc[k][b], whole * src[3 + k]) - m * src[k]
            for b in range(blocks):
                top = start + 8 * b
                for k in range(4):
                    sums[top : top + 8, k : k + 1] = jnp.sum(acc[k][b], axis=1, keepdims=True)
        flat = sums[...].T[0:4, :points]
        out_ref[j] = flat[0:3] + own_ref[0:3, :points] * flat[3:4] + wall_ref[j]

    def step(j, s_ref, r_ref, w_ref, own_ref, a_ref):
        center = prepare_own(j, point_ref, density_ref, weight_ref, feature_ref, own_ref, a_ref, 2)
        prepare(j, center, r_ref, w_ref)
        products(a_ref, w_ref, s_ref)

    start_features(feature_ref)
    step(0, s0, r0, w0, o0, a0)

    def body(i, carry):
        j = 2 * i
        step(j + 1, s1, r1, w1, o1, a1)
        evaluate(j, s0, r0, o0)
        step(jnp.minimum(j + 2, cells - 1), s0, r0, w0, o0, a0)
        evaluate(j + 1, s1, r1, o1)
        return carry

    lax.fori_loop(0, cells // 2, body, 0)


def wall_kernel(
    ids_ref,
    patch_ref,
    point_ref,
    density_ref,
    weight_ref,
    out_ref,
    back_ref,
    s0,
    s1,
    r0,
    r1,
    w0,
    w1,
    o0,
    o1,
    a0,
    a1,
    feature_ref,
    sums,
    columns,
):
    cells = out_ref.shape[0]
    points = out_ref.shape[2]
    tiles = r0.shape[1] // lanes
    lane = lax.broadcasted_iota(jnp.int32, (8, lanes), 1)
    back_ref[...] = jnp.zeros_like(back_ref)

    def prepare(j, center, r_ref, w_ref):
        parts = []
        for t in range(tiles):
            left, right = ids_ref[j, 2 * t], ids_ref[j, 2 * t + 1]
            one = pltpu.roll(patch_ref[left // 2], 64 * (left % 2), 1)
            two = pltpu.roll(patch_ref[right // 2], 64 * (1 - right % 2), 1)
            parts.append(jnp.where(lane < 64, one, two) - center)
        raw = jnp.concatenate(parts, axis=1)
        r_ref[...] = raw
        w_ref[...] = source_features(raw)

    def evaluate(j, s_ref, r_ref, own_ref):
        blocks = 2
        columns[...] = own_ref[...].T
        back = [[None] * 4 for _ in range(tiles)]
        for start in range(0, points, 8 * blocks):
            acc = [[None] * blocks for _ in range(4)]
            own = [
                [
                    jnp.broadcast_to(columns[start + 8 * b : start + 8 * b + 8, k : k + 1], (8, lanes))
                    for k in range(6)
                ]
                for b in range(blocks)
            ]
            for c in range(tiles):
                cols = slice(c * lanes, c * lanes + lanes)
                src = source_rows(r_ref, cols)
                for b in range(blocks):
                    top = start + 8 * b
                    h = lax.rsqrt(s_ref[top : top + 8, cols])
                    cube = h * h * h
                    whole = h + cube
                    m = s_ref[points + top : points + top + 8, cols] * cube
                    n = s_ref[2 * points + top : 2 * points + top + 8, cols] * cube
                    acc[3][b] = added(acc[3][b], m)
                    back[c][3] = added(back[c][3], n)
                    for k in range(3):
                        acc[k][b] = added(acc[k][b], whole * src[3 + k]) - m * src[k]
                        back[c][k] = added(back[c][k], whole * own[b][3 + k]) - n * own[b][k]
            for b in range(blocks):
                top = start + 8 * b
                for k in range(4):
                    sums[top : top + 8, k : k + 1] = jnp.sum(acc[k][b], axis=1, keepdims=True)
        flat = sums[...].T[0:4, :points]
        out_ref[j] = flat[0:3] + own_ref[0:3, :points] * flat[3:4]
        for c in range(tiles):
            rows = [jnp.sum(back[c][k], axis=0, keepdims=True) for k in range(4)]
            rows = jnp.concatenate(rows + [jnp.zeros((4, lanes), f32)], axis=0)
            term = rows + r_ref[:, c * lanes : c * lanes + lanes] * rows[3:4, :]
            for half in range(2):
                patch = ids_ref[j, 2 * c + half]
                odd = patch % 2
                moved = pltpu.roll(term, 64 * (odd if half == 0 else 1 - odd), 1)
                kept = jnp.where((lane >= 64) == (odd == 1), moved, 0.0)
                back_ref[patch // 2] += kept

    def step(j, s_ref, r_ref, w_ref, own_ref, a_ref):
        center = prepare_own(j, point_ref, density_ref, weight_ref, feature_ref, own_ref, a_ref, 3)
        prepare(j, center, r_ref, w_ref)
        products(a_ref, w_ref, s_ref)

    start_features(feature_ref)
    own_ref_rows = jnp.zeros_like(o0)
    o0[...] = own_ref_rows
    o1[...] = own_ref_rows
    step(0, s0, r0, w0, o0, a0)

    def body(i, carry):
        j = 2 * i
        step(j + 1, s1, r1, w1, o1, a1)
        evaluate(j, s0, r0, o0)
        step(jnp.minimum(j + 2, cells - 1), s0, r0, w0, o0, a0)
        evaluate(j + 1, s1, r1, o1)
        return carry

    lax.fori_loop(0, cells // 2, body, 0)


def scratch(points, kinds, tiles):
    wide = -(-points // lanes) * lanes
    return [
        pltpu.VMEM((kinds * points, tiles * lanes), f32),
        pltpu.VMEM((kinds * points, tiles * lanes), f32),
        pltpu.VMEM((8, tiles * lanes), f32),
        pltpu.VMEM((8, tiles * lanes), f32),
        pltpu.VMEM((depth, tiles * lanes), bf16),
        pltpu.VMEM((depth, tiles * lanes), bf16),
        pltpu.VMEM((8, wide), f32),
        pltpu.VMEM((8, wide), f32),
        pltpu.VMEM((kinds * points, depth), bf16),
        pltpu.VMEM((kinds * points, depth), bf16),
        pltpu.VMEM((kinds * depth, wide), f32),
        pltpu.VMEM((wide, lanes), f32),
    ]


def local(
    cell_points,
    cell_density,
    cell_weights,
    near_device,
    near_slot,
    near_wall,
    wall_points,
    wall_density,
    wall_weights,
):
    wall_count = lax.axis_size("wall")
    wall_index = lax.axis_index("wall")
    cells, _, points = cell_points.shape
    patch_dev, _, patch_pts = wall_points.shape
    quarter = points // wall_count
    extra = quarter - lanes
    part = patch_pts // wall_count
    wide = -(-points // lanes) * lanes
    vmem = pl.BlockSpec(memory_space=pltpu.VMEM)
    smem = pl.BlockSpec(memory_space=pltpu.SMEM)
    params = pltpu.CompilerParams(vmem_limit_bytes=60 * 2**20)

    cell_load = cell_density * cell_weights[:, None, :]
    raw = jnp.concatenate([2.0 * cell_points, cell_load], axis=1)
    mine = lax.dynamic_slice_in_dim(raw, wall_index * quarter, quarter, 2)
    gap = jnp.zeros((cells, lanes - 6 * extra), f32)
    ends = [mine[:, q, lanes:] for q in range(6)]
    tail = jnp.concatenate([ends[0], gap] + ends[:0:-1], axis=1)[:, None, :]
    block = jnp.concatenate([mine[:, :, :lanes], tail, jnp.zeros((cells, 1, lanes), f32)], axis=1)
    gathered = lax.all_gather(block, "cell", axis=0, tiled=True)

    wall_raw = jnp.concatenate(
        [2.0 * wall_points, wall_density * wall_weights[:, None, :], jnp.zeros((patch_dev, 2, patch_pts), f32)],
        axis=1,
    )
    wall_raw = wall_raw.reshape(patch_dev // 2, 2, 8, wall_count, part).transpose(3, 0, 2, 1, 4)
    wall_raw = wall_raw.reshape(wall_count * (patch_dev // 2), 8, 2 * part)
    patches = lax.all_to_all(wall_raw, "wall", split_axis=0, concat_axis=0, tiled=True)

    tiles = near_wall.shape[1] * part // lanes
    wall_term, back = pl.pallas_call(
        wall_kernel,
        out_shape=(
            jax.ShapeDtypeStruct((cells, 3, points), f32),
            jax.ShapeDtypeStruct(patches.shape, f32),
        ),
        in_specs=[smem] + [vmem] * 4,
        out_specs=(vmem, vmem),
        scratch_shapes=scratch(points, 3, tiles) + [pltpu.VMEM((wide, 8), f32)],
        compiler_params=params,
        cost_estimate=pl.CostEstimate(flops=10**9, bytes_accessed=10**8, transcendentals=0),
        name="wall_pairs",
    )(near_wall, patches, cell_points, cell_density, cell_weights)

    near_ids = near_device * cells + near_slot
    tiles = near_device.shape[1] + 1
    total = pl.pallas_call(
        near_kernel,
        out_shape=jax.ShapeDtypeStruct((cells, 3, points), f32),
        in_specs=[smem] + [vmem] * 5,
        out_specs=vmem,
        scratch_shapes=scratch(points, 2, tiles),
        compiler_params=params,
        cost_estimate=pl.CostEstimate(flops=10**9, bytes_accessed=10**8, transcendentals=0),
        name="near_pairs",
    )(near_ids, gathered, cell_points, cell_density, cell_weights, wall_term)

    total = total.reshape(cells, 3, wall_count, quarter).transpose(2, 0, 1, 3)
    share = jnp.sum(lax.all_to_all(total, "wall", split_axis=0, concat_axis=0, tiled=True), axis=0)
    own = lax.dynamic_slice_in_dim(cell_density, wall_index * quarter, quarter, 2)
    velocity = 0.5 * own + two_stokes_factor * share

    back = lax.all_to_all(back[:, :3, :], "wall", split_axis=0, concat_axis=0, tiled=True)
    back = back.reshape(wall_count, patch_dev // 2, 3, 2, part).transpose(1, 3, 2, 0, 4)
    wall_velocity = 0.5 * wall_density + two_stokes_factor * back.reshape(patch_dev, 3, patch_pts)
    return (velocity, wall_velocity)


def solution(mesh):
    in_specs = (
        P("cell", None, None),
        P("cell", None, None),
        P("cell", None),
        P("cell", None),
        P("cell", None),
        P("cell", None),
        P(("cell", "wall"), None, None),
        P(("cell", "wall"), None, None),
        P(("cell", "wall"), None),
    )
    out_specs = (P("cell", None, "wall"), P(("cell", "wall"), None, None))
    return jax.shard_map(local, mesh=mesh, in_specs=in_specs, out_specs=out_specs, check_vma=False)
```

```python
import jax
import jax.numpy as jnp
from jax import lax
from jax.experimental import pallas as pl
from jax.experimental.pallas import tpu as pltpu
from jax.sharding import PartitionSpec as P

f32 = jnp.float32
bf16 = jnp.bfloat16
two_stokes_factor = 2.0 * 0.039788735772973836
levels = ((1, 1), (1, 2), (1, 3), (2, 1), (2, 2), (3, 1))
depth = 64
lanes = 128


def split3(x):
    first = x.astype(bf16).astype(f32)
    rest = x - first
    second = rest.astype(bf16).astype(f32)
    return first, second, rest - second


def source_features(raw):
    y = [raw[i : i + 1, :] for i in range(3)]
    g = [raw[i : i + 1, :] for i in range(3, 6)]
    square = y[0] * y[0] + y[1] * y[1] + y[2] * y[2] + 1.0
    dot = g[0] * y[0] + g[1] * y[1] + g[2] * y[2]
    rows = jnp.concatenate(
        [-2.0 * y[0], -2.0 * y[1], -2.0 * y[2], square, g[0], g[1], g[2], -dot], axis=0
    )
    parts = split3(rows)
    one = jnp.ones_like(rows)
    stack = [parts[p - 1] for p, _ in levels] + [one, jnp.zeros_like(rows)]
    return jnp.concatenate(stack, axis=0).astype(bf16)


def own_kernel(point_ref, density_ref, weight_ref, target_ref, own_ref, center_ref, feature_ref):
    points = point_ref.shape[2]
    first = pl.program_id(0) * point_ref.shape[0]
    start_features(feature_ref)

    def cell(i, carry):
        x = 2.0 * point_ref[i]
        center = jnp.sum(x, axis=1, keepdims=True) * (1.0 / points)
        x = x - center
        load = density_ref[i] * weight_ref[pl.ds(first + i, 1), :]
        own_ref[i] = jnp.zeros(own_ref.shape[1:], f32)
        own_ref[i, 0:3, :points] = x
        own_ref[i, 3:6, :points] = load
        xs, ls = split3(x), split3(-0.5 * load)
        squares = split3(jnp.sum(x * x, axis=0, keepdims=True))
        dots = split3(-jnp.sum(x * load, axis=0, keepdims=True))
        for n, (_, q) in enumerate(levels):
            feature_ref[8 * n : 8 * n + 3, :points] = xs[q - 1]
            feature_ref[depth + 8 * n + 4 : depth + 8 * n + 7, :points] = xs[q - 1]
            feature_ref[2 * depth + 8 * n : 2 * depth + 8 * n + 3, :points] = ls[q - 1]
        for n in range(3):
            feature_ref[48 + n : 49 + n, :points] = squares[n]
            feature_ref[2 * depth + 48 + n : 2 * depth + 49 + n, :points] = dots[n]
        for kind in range(3):
            turned = feature_ref[kind * depth : kind * depth + depth, :].T
            target_ref[i, kind * points : kind * points + points, :] = turned[:points].astype(bf16)
        center_ref[i] = jnp.concatenate(
            [jnp.broadcast_to(center, (3, lanes)), jnp.zeros((5, lanes), f32)], axis=0
        )
        return carry

    lax.fori_loop(0, point_ref.shape[0], cell, 0)


def start_features(feature_ref):
    feature_ref[...] = jnp.zeros_like(feature_ref)
    one = jnp.ones((1, feature_ref.shape[1]), f32)
    for i, (_, q) in enumerate(levels):
        if q == 1:
            feature_ref[8 * i + 3 : 8 * i + 4, :] = one
            feature_ref[depth + 8 * i + 7 : depth + 8 * i + 8, :] = one


def product_tiles(a_ref, w_ref, s_ref):
    n = w_ref.shape[1]

    def tile(c):
        e = min(n, c + 256)
        s_ref[:, c:e] = jnp.dot(a_ref[...], w_ref[:, c:e], preferred_element_type=f32)

    return [lambda c=c: tile(c) for c in range(0, n, 256)]


def source_rows(r_ref, cols):
    return [jnp.broadcast_to(r_ref[i : i + 1, cols], (8, lanes)) for i in range(6)]


def added(total, term):
    return term if total is None else total + term


def woven(main, side):
    done = 0
    for i, piece in enumerate(main):
        while done < len(side) and done * len(main) <= i * len(side):
            side[done]()
            done += 1
        piece()
    for piece in side[done:]:
        piece()


def keep_sums(acc, top, acc_ref):
    for k in range(4):
        rows = jnp.concatenate(acc[k], axis=0)
        high = rows.astype(bf16)
        low = (rows - high.astype(f32)).astype(bf16)
        acc_ref[top : top + rows.shape[0], 2 * k * lanes : (2 * k + 1) * lanes] = high
        acc_ref[top : top + rows.shape[0], (2 * k + 1) * lanes : (2 * k + 2) * lanes] = low


def finish_pieces(j, acc_ref, own_ref, fold_ref, out_ref, more_ref):
    points = out_ref.shape[2]

    def fold():
        flat = lax.dot_general(
            fold_ref[...], acc_ref[...], (((1,), (1,)), ((), ())), preferred_element_type=f32
        )
        total = flat[0:3] + own_ref[j, 0:3, :points] * flat[3:4]
        out_ref[j] = total if more_ref is None else total + more_ref[j]

    return [fold]


def start_fold(fold_ref):
    row = lax.broadcasted_iota(jnp.int32, fold_ref.shape, 0)
    column = lax.broadcasted_iota(jnp.int32, fold_ref.shape, 1)
    fold_ref[...] = jnp.where(row == column // (2 * lanes), 1.0, 0.0).astype(bf16)


def near_kernel(
    ids_ref,
    gathered_ref,
    own_ref,
    center_ref,
    target_ref,
    wall_ref,
    out_ref,
    s0,
    s1,
    r0,
    r1,
    w0,
    w1,
    a0,
    a1,
    c0,
    c1,
    fold_ref,
    copied,
):
    cells = out_ref.shape[0]
    points = out_ref.shape[2]
    tiles = r0.shape[1] // lanes
    blocks = 4

    def prepare(j, r_ref, w_ref):
        center = center_ref[j]
        lane = lax.broadcasted_iota(jnp.int32, (8, lanes), 1)
        tail = jnp.zeros((8, lanes), f32)
        parts = []
        for k in range(8):
            block = gathered_ref[ids_ref[j, k]]
            parts.append(block - center)
            last = jnp.broadcast_to(block[6:7, :], (8, lanes))
            last = pltpu.roll(last, 8 * k, 1, stride=8, stride_axis=0)
            tail = jnp.where((lane >= 8 * k) & (lane < 8 * k + 8), last, tail)
        parts.append(jnp.where(lane < 64, tail - center, 0.0))
        raw = jnp.concatenate(parts, axis=1)
        r_ref[...] = raw
        w_ref[...] = source_features(raw)

    def chunk(start, s_ref, r_ref, acc_ref):
        acc = [[None] * blocks for _ in range(4)]
        for c in range(tiles):
            cols = slice(c * lanes, c * lanes + lanes)
            src = source_rows(r_ref, cols)
            for b in range(blocks):
                top = start + 8 * b
                h = lax.rsqrt(s_ref[top : top + 8, cols])
                cube = h * h * h
                whole = h + cube
                m = s_ref[points + top : points + top + 8, cols] * cube
                acc[3][b] = added(acc[3][b], m)
                for k in range(3):
                    acc[k][b] = added(acc[k][b], whole * src[3 + k]) - m * src[k]
        keep_sums(acc, start, acc_ref)

    def fetch(j, slot):
        a_ref = (a0, a1)[slot]
        source = target_ref.at[jnp.minimum(j, cells - 1), pl.ds(0, a_ref.shape[0])]
        return pltpu.make_async_copy(source, a_ref, copied.at[slot])

    def stage(j, slot, last):
        s_ref, r_ref, w_ref, a_ref, acc_ref = sets[slot]
        next_s, next_r, next_w, next_a, next_acc = sets[1 - slot]
        fetch(j + 2, slot).start()
        fetch(j + 1, 1 - slot).wait()
        side = finish_pieces(jnp.maximum(j - 1, 0), next_acc, own_ref, fold_ref, out_ref, wall_ref)
        side += [lambda: prepare(last, next_r, next_w)]
        side += product_tiles(next_a, next_w, next_s)
        main = [lambda t=t: chunk(t, s_ref, r_ref, acc_ref) for t in range(0, points, 8 * blocks)]
        woven(main, side)

    sets = ((s0, r0, w0, a0, c0), (s1, r1, w1, a1, c1))
    start_fold(fold_ref)
    c1[...] = jnp.zeros_like(c1)
    fetch(0, 0).start()
    fetch(1, 1).start()
    prepare(0, r0, w0)
    fetch(0, 0).wait()
    for piece in product_tiles(a0, w0, s0):
        piece()

    def body(i, carry):
        j = 2 * i
        stage(j, 0, j + 1)
        stage(j + 1, 1, jnp.minimum(j + 2, cells - 1))
        return carry

    lax.fori_loop(0, cells // 2, body, 0)
    fetch(cells + 1, 1).wait()
    for piece in finish_pieces(cells - 1, c1, own_ref, fold_ref, out_ref, wall_ref):
        piece()


def wall_kernel(
    ids_ref,
    patch_ref,
    own_ref,
    center_ref,
    target_ref,
    out_ref,
    back_ref,
    s0,
    s1,
    r0,
    r1,
    w0,
    w1,
    a0,
    a1,
    c0,
    c1,
    fold_ref,
    copied,
    p0,
    p1,
    pick_ref,
):
    cells = out_ref.shape[0]
    points = out_ref.shape[2]
    tiles = r0.shape[1] // lanes
    blocks = 2
    lane = lax.broadcasted_iota(jnp.int32, (8, lanes), 1)

    def prepare(j, r_ref, w_ref):
        center = center_ref[j]
        parts = []
        for t in range(tiles):
            left, right = ids_ref[j, 2 * t], ids_ref[j, 2 * t + 1]
            one = pltpu.roll(patch_ref[left // 2], 64 * (left % 2), 1)
            two = pltpu.roll(patch_ref[right // 2], 64 * (1 - right % 2), 1)
            parts.append(jnp.where(lane < 64, one, two) - center)
        raw = jnp.concatenate(parts, axis=1)
        r_ref[...] = raw
        w_ref[...] = source_features(raw)

    def chunk(start, s_ref, r_ref, acc_ref, p_ref, back):
        acc = [[None] * blocks for _ in range(4)]
        own = [
            [p_ref[start + 8 * b : start + 8 * b + 8, k * lanes : k * lanes + lanes] for k in range(6)]
            for b in range(blocks)
        ]
        for c in range(tiles):
            cols = slice(c * lanes, c * lanes + lanes)
            src = source_rows(r_ref, cols)
            for b in range(blocks):
                top = start + 8 * b
                h = lax.rsqrt(s_ref[top : top + 8, cols])
                cube = h * h * h
                whole = h + cube
                m = s_ref[points + top : points + top + 8, cols] * cube
                n = s_ref[2 * points + top : 2 * points + top + 8, cols] * cube
                acc[3][b] = added(acc[3][b], m)
                back[c][3] = added(back[c][3], n)
                for k in range(3):
                    acc[k][b] = added(acc[k][b], whole * src[3 + k]) - m * src[k]
                    back[c][k] = added(back[c][k], whole * own[b][3 + k]) - n * own[b][k]
        keep_sums(acc, start, acc_ref)

    def give_back(j, r_ref, back):
        for c in range(tiles):
            rows = [jnp.sum(back[c][k], axis=0, keepdims=True) for k in range(4)]
            rows = jnp.concatenate(rows + [jnp.zeros((4, lanes), f32)], axis=0)
            term = rows + r_ref[:, c * lanes : c * lanes + lanes] * rows[3:4, :]
            for half in range(2):
                patch = ids_ref[j, 2 * c + half]
                odd = patch % 2
                moved = pltpu.roll(term, 64 * (odd if half == 0 else 1 - odd), 1)
                kept = jnp.where((lane >= 64) == (odd == 1), moved, 0.0)
                back_ref[patch // 2] += kept

    def fetch(j, slot):
        a_ref = (a0, a1)[slot]
        source = target_ref.at[jnp.minimum(j, cells - 1), pl.ds(0, a_ref.shape[0])]
        return pltpu.make_async_copy(source, a_ref, copied.at[slot])

    def spread_pieces(a_ref, p_ref):
        half = 3 * lanes

        def positions():
            p_ref[:, :half] = jnp.dot(a_ref[:points], pick_ref[:, :half], preferred_element_type=f32)

        def loads():
            p_ref[:, half:] = jnp.dot(a_ref[2 * points :], pick_ref[:, half:], preferred_element_type=f32)

        return [positions, loads]

    def stage(j, slot, last):
        s_ref, r_ref, w_ref, a_ref, acc_ref, p_ref = sets[slot]
        next_s, next_r, next_w, next_a, next_acc, next_p = sets[1 - slot]
        fetch(j + 2, slot).start()
        fetch(j + 1, 1 - slot).wait()
        side = finish_pieces(jnp.maximum(j - 1, 0), next_acc, own_ref, fold_ref, out_ref, None)
        side += [lambda: prepare(last, next_r, next_w)]
        side += product_tiles(next_a, next_w, next_s) + spread_pieces(next_a, next_p)
        back = [[None] * 4 for _ in range(tiles)]
        main = [lambda t=t: chunk(t, s_ref, r_ref, acc_ref, p_ref, back) for t in range(0, points, 8 * blocks)]
        woven(main, side)
        give_back(j, r_ref, back)

    sets = ((s0, r0, w0, a0, c0, p0), (s1, r1, w1, a1, c1, p1))
    back_ref[...] = jnp.zeros_like(back_ref)
    start_fold(fold_ref)
    feature = lax.broadcasted_iota(jnp.int32, pick_ref.shape, 0)
    column = lax.broadcasted_iota(jnp.int32, pick_ref.shape, 1) // lanes
    hit = (feature < 24) & (feature % 8 == column % 3)
    pick_ref[...] = jnp.where(hit, jnp.where(column < 3, 1.0, -2.0), 0.0).astype(bf16)
    c1[...] = jnp.zeros_like(c1)
    fetch(0, 0).start()
    fetch(1, 1).start()
    prepare(0, r0, w0)
    fetch(0, 0).wait()
    for piece in product_tiles(a0, w0, s0) + spread_pieces(a0, p0):
        piece()

    def body(i, carry):
        j = 2 * i
        stage(j, 0, j + 1)
        stage(j + 1, 1, jnp.minimum(j + 2, cells - 1))
        return carry

    lax.fori_loop(0, cells // 2, body, 0)
    fetch(cells + 1, 1).wait()
    for piece in finish_pieces(cells - 1, c1, own_ref, fold_ref, out_ref, None):
        piece()


def scratch(points, kinds, tiles):
    pairs = [
        pltpu.VMEM((kinds * points, tiles * lanes), f32),
        pltpu.VMEM((8, tiles * lanes), f32),
        pltpu.VMEM((depth, tiles * lanes), bf16),
        pltpu.VMEM((kinds * points, depth), bf16),
        pltpu.VMEM((points, 8 * lanes), bf16),
    ]
    shapes = [shape for shape in pairs for _ in range(2)]
    shapes += [pltpu.VMEM((16, 8 * lanes), bf16), pltpu.SemaphoreType.DMA((2,))]
    if kinds == 3:
        shapes += [pltpu.VMEM((points, 6 * lanes), f32)] * 2 + [pltpu.VMEM((depth, 6 * lanes), bf16)]
    return shapes


def local(
    cell_points,
    cell_density,
    cell_weights,
    near_device,
    near_slot,
    near_wall,
    wall_points,
    wall_density,
    wall_weights,
):
    wall_count = lax.axis_size("wall")
    wall_index = lax.axis_index("wall")
    cells, _, points = cell_points.shape
    patch_dev, _, patch_pts = wall_points.shape
    quarter = points // wall_count
    extra = quarter - lanes
    part = patch_pts // wall_count
    vmem = pl.BlockSpec(memory_space=pltpu.VMEM)
    smem = pl.BlockSpec(memory_space=pltpu.SMEM)
    hbm = pl.BlockSpec(memory_space=pl.ANY)
    params = pltpu.CompilerParams(vmem_limit_bytes=60 * 2**20)

    cell_load = cell_density * cell_weights[:, None, :]
    raw = jnp.concatenate([2.0 * cell_points, cell_load], axis=1)
    mine = lax.dynamic_slice_in_dim(raw, wall_index * quarter, quarter, 2)
    gap = jnp.zeros((cells, lanes - 6 * extra), f32)
    ends = [mine[:, q, lanes:] for q in range(6)]
    tail = jnp.concatenate([ends[0], gap] + ends[:0:-1], axis=1)[:, None, :]
    block = jnp.concatenate([mine[:, :, :lanes], tail, jnp.zeros((cells, 1, lanes), f32)], axis=1)
    gathered = lax.all_gather(block, "cell", axis=0, tiled=True)

    wall_raw = jnp.concatenate(
        [2.0 * wall_points, wall_density * wall_weights[:, None, :], jnp.zeros((patch_dev, 2, patch_pts), f32)],
        axis=1,
    )
    wall_raw = wall_raw.reshape(patch_dev // 2, 2, 8, wall_count, part).transpose(3, 0, 2, 1, 4)
    wall_raw = wall_raw.reshape(wall_count * (patch_dev // 2), 8, 2 * part)
    patches = lax.all_to_all(wall_raw, "wall", split_axis=0, concat_axis=0, tiled=True)

    wide = -(-points // lanes) * lanes
    batch = 4

    def by_batch(*shape):
        return pl.BlockSpec((batch,) + shape, lambda i: (i, 0, 0))

    target, own_rows, center = pl.pallas_call(
        own_kernel,
        grid=(cells // batch,),
        out_shape=(
            jax.ShapeDtypeStruct((cells, 3 * points, depth), bf16),
            jax.ShapeDtypeStruct((cells, 8, wide), f32),
            jax.ShapeDtypeStruct((cells, 8, lanes), f32),
        ),
        in_specs=[by_batch(3, points), by_batch(3, points), vmem],
        out_specs=(by_batch(3 * points, depth), by_batch(8, wide), by_batch(8, lanes)),
        scratch_shapes=[pltpu.VMEM((3 * depth, wide), f32)],
        compiler_params=pltpu.CompilerParams(vmem_limit_bytes=24 * 2**20),
        cost_estimate=pl.CostEstimate(flops=10**7, bytes_accessed=2 * 10**7, transcendentals=0),
        name="own_features",
    )(cell_points, cell_density, cell_weights)

    tiles = near_wall.shape[1] * part // lanes
    wall_term, back = pl.pallas_call(
        wall_kernel,
        out_shape=(
            jax.ShapeDtypeStruct((cells, 3, points), f32),
            jax.ShapeDtypeStruct(patches.shape, f32),
        ),
        in_specs=[smem] + [vmem] * 3 + [hbm],
        out_specs=(vmem, vmem),
        scratch_shapes=scratch(points, 3, tiles),
        compiler_params=params,
        cost_estimate=pl.CostEstimate(flops=10**9, bytes_accessed=10**8, transcendentals=0),
        name="wall_pairs",
    )(near_wall, patches, own_rows, center, target)

    near_ids = near_device * cells + near_slot
    tiles = near_device.shape[1] + 1
    total = pl.pallas_call(
        near_kernel,
        out_shape=jax.ShapeDtypeStruct((cells, 3, points), f32),
        in_specs=[smem] + [vmem] * 3 + [hbm, vmem],
        out_specs=vmem,
        scratch_shapes=scratch(points, 2, tiles),
        compiler_params=params,
        cost_estimate=pl.CostEstimate(flops=10**9, bytes_accessed=10**8, transcendentals=0),
        name="near_pairs",
    )(near_ids, gathered, own_rows, center, target, wall_term)

    total = total.reshape(cells, 3, wall_count, quarter).transpose(2, 0, 1, 3)
    share = jnp.sum(lax.all_to_all(total, "wall", split_axis=0, concat_axis=0, tiled=True), axis=0)
    own = lax.dynamic_slice_in_dim(cell_density, wall_index * quarter, quarter, 2)
    velocity = 0.5 * own + two_stokes_factor * share

    back = lax.all_to_all(back[:, :3, :], "wall", split_axis=0, concat_axis=0, tiled=True)
    back = back.reshape(wall_count, patch_dev // 2, 3, 2, part).transpose(1, 3, 2, 0, 4)
    wall_velocity = 0.5 * wall_density + two_stokes_factor * back.reshape(patch_dev, 3, patch_pts)
    return (velocity, wall_velocity)


def solution(mesh):
    in_specs = (
        P("cell", None, None),
        P("cell", None, None),
        P("cell", None),
        P("cell", None),
        P("cell", None),
        P("cell", None),
        P(("cell", "wall"), None, None),
        P(("cell", "wall"), None, None),
        P(("cell", "wall"), None),
    )
    out_specs = (P("cell", None, "wall"), P(("cell", "wall"), None, None))
    return jax.shard_map(local, mesh=mesh, in_specs=in_specs, out_specs=out_specs, check_vma=False)
```

```python
import jax
import jax.numpy as jnp
from jax import lax
from jax.experimental import pallas as pl
from jax.experimental.pallas import tpu as pltpu
from jax.sharding import PartitionSpec as P

f32 = jnp.float32
bf16 = jnp.bfloat16
two_stokes_factor = 2.0 * 0.039788735772973836
levels = ((1, 1), (1, 2), (1, 3), (2, 1), (2, 2), (3, 1))
depth = 64
lanes = 128


def split3(x):
    first = x.astype(bf16).astype(f32)
    rest = x - first
    second = rest.astype(bf16).astype(f32)
    return first, second, rest - second


def source_features(raw):
    y = [raw[i : i + 1, :] for i in range(3)]
    g = [raw[i : i + 1, :] for i in range(3, 6)]
    square = y[0] * y[0] + y[1] * y[1] + y[2] * y[2] + 1.0
    dot = g[0] * y[0] + g[1] * y[1] + g[2] * y[2]
    rows = jnp.concatenate(
        [-2.0 * y[0], -2.0 * y[1], -2.0 * y[2], square, g[0], g[1], g[2], -dot], axis=0
    )
    parts = split3(rows)
    one = jnp.ones_like(rows)
    stack = [parts[p - 1] for p, _ in levels] + [one, jnp.zeros_like(rows)]
    return jnp.concatenate(stack, axis=0).astype(bf16)


def prepare_own(j, point_ref, density_ref, weight_ref, feature_ref, own_ref, a_ref, kinds):
    points = point_ref.shape[2]
    x = 2.0 * point_ref[j]
    center = jnp.sum(x, axis=1, keepdims=True) * (1.0 / points)
    x = x - center
    load = density_ref[j] * weight_ref[pl.ds(j, 1), :]
    own_ref[0:3, :points] = x
    own_ref[3:6, :points] = load
    xs = split3(x)
    squares = split3(jnp.sum(x * x, axis=0, keepdims=True))
    for i, (_, q) in enumerate(levels):
        feature_ref[8 * i : 8 * i + 3, :points] = xs[q - 1]
        feature_ref[depth + 8 * i + 4 : depth + 8 * i + 7, :points] = xs[q - 1]
    for i in range(3):
        feature_ref[48 + i : 49 + i, :points] = squares[i]
    if kinds == 3:
        ls = split3(-0.5 * load)
        dots = split3(-jnp.sum(x * load, axis=0, keepdims=True))
        for i, (_, q) in enumerate(levels):
            feature_ref[2 * depth + 8 * i : 2 * depth + 8 * i + 3, :points] = ls[q - 1]
        for i in range(3):
            feature_ref[2 * depth + 48 + i : 2 * depth + 49 + i, :points] = dots[i]
    for kind in range(kinds):
        turned = feature_ref[kind * depth : kind * depth + depth, :].T
        a_ref[kind * points : kind * points + points, :] = turned[:points].astype(bf16)
    return jnp.concatenate([jnp.broadcast_to(center, (3, lanes)), jnp.zeros((5, lanes), f32)], axis=0)


def start_features(feature_ref):
    feature_ref[...] = jnp.zeros_like(feature_ref)
    one = jnp.ones((1, feature_ref.shape[1]), f32)
    for i, (_, q) in enumerate(levels):
        if q == 1:
            feature_ref[8 * i + 3 : 8 * i + 4, :] = one
            feature_ref[depth + 8 * i + 7 : depth + 8 * i + 8, :] = one


def product_tiles(a_ref, w_ref, s_ref):
    n = w_ref.shape[1]

    def tile(c):
        e = min(n, c + 256)
        s_ref[:, c:e] = jnp.dot(a_ref[...], w_ref[:, c:e], preferred_element_type=f32)

    return [lambda c=c: tile(c) for c in range(0, n, 256)]


def source_rows(r_ref, cols):
    return [jnp.broadcast_to(r_ref[i : i + 1, cols], (8, lanes)) for i in range(6)]


def added(total, term):
    return term if total is None else total + term


def woven(main, side):
    done = 0
    for i, piece in enumerate(main):
        while done < len(side) and done * len(main) <= i * len(side):
            side[done]()
            done += 1
        piece()
    for piece in side[done:]:
        piece()


def finish_pieces(j, acc_ref, own_ref, out_ref, more_ref):
    points = out_ref.shape[2]

    def turn():
        turned = acc_ref[...].T
        if more_ref is None:
            out_ref[j] = turned[0:3, :points]
        else:
            out_ref[j] = turned[0:3, :points] + own_ref[0:3, :points] * turned[3:4, :points] + more_ref[j]

    return [turn]


def near_kernel(
    ids_ref,
    gathered_ref,
    point_ref,
    density_ref,
    weight_ref,
    wall_ref,
    out_ref,
    s0,
    s1,
    r0,
    r1,
    w0,
    w1,
    o0,
    o1,
    a0,
    a1,
    c0,
    c1,
    feature_ref,
):
    cells = out_ref.shape[0]
    points = out_ref.shape[2]
    tiles = r0.shape[1] // lanes
    blocks = 4

    def prepare(j, center, r_ref, w_ref):
        lane = lax.broadcasted_iota(jnp.int32, (8, lanes), 1)
        tail = jnp.zeros((8, lanes), f32)
        parts = []
        for k in range(8):
            block = gathered_ref[ids_ref[j, k]]
            parts.append(block - center)
            last = jnp.broadcast_to(block[6:7, :], (8, lanes))
            last = pltpu.roll(last, 8 * k, 1, stride=8, stride_axis=0)
            tail = jnp.where((lane >= 8 * k) & (lane < 8 * k + 8), last, tail)
        parts.append(jnp.where(lane < 64, tail - center, 0.0))
        raw = jnp.concatenate(parts, axis=1)
        r_ref[...] = raw
        w_ref[...] = source_features(raw)

    def chunk(start, s_ref, r_ref, acc_ref):
        acc = [[None] * blocks for _ in range(4)]
        for c in range(tiles):
            cols = slice(c * lanes, c * lanes + lanes)
            src = source_rows(r_ref, cols)
            for b in range(blocks):
                top = start + 8 * b
                h = lax.rsqrt(s_ref[top : top + 8, cols])
                cube = h * h * h
                whole = h + cube
                m = s_ref[points + top : points + top + 8, cols] * cube
                acc[3][b] = added(acc[3][b], m)
                for k in range(3):
                    acc[k][b] = added(acc[k][b], whole * src[3 + k]) - m * src[k]
        for b in range(blocks):
            top = start + 8 * b
            for k in range(4):
                acc_ref[top : top + 8, k : k + 1] = jnp.sum(acc[k][b], axis=1, keepdims=True)

    def step(j, r_ref, w_ref, own_ref, a_ref):
        center = prepare_own(j, point_ref, density_ref, weight_ref, feature_ref, own_ref, a_ref, 2)
        prepare(j, center, r_ref, w_ref)

    def stage(j, now, later, last):
        s_ref, r_ref, w_ref, own_ref, a_ref, acc_ref = now
        next_s, next_r, next_w, next_own, next_a, next_acc = later
        side = finish_pieces(jnp.maximum(j - 1, 0), next_acc, next_own, out_ref, wall_ref)
        side += [lambda: step(last, next_r, next_w, next_own, next_a)]
        side += product_tiles(next_a, next_w, next_s)
        main = [lambda t=t: chunk(t, s_ref, r_ref, acc_ref) for t in range(0, points, 8 * blocks)]
        woven(main, side)

    even = (s0, r0, w0, o0, a0, c0)
    odd = (s1, r1, w1, o1, a1, c1)
    start_features(feature_ref)
    c0[...] = jnp.zeros_like(c0)
    c1[...] = jnp.zeros_like(c1)
    o1[...] = jnp.zeros_like(o1)
    step(0, r0, w0, o0, a0)
    for piece in product_tiles(a0, w0, s0):
        piece()

    def body(i, carry):
        j = 2 * i
        stage(j, even, odd, j + 1)
        stage(j + 1, odd, even, jnp.minimum(j + 2, cells - 1))
        return carry

    lax.fori_loop(0, cells // 2, body, 0)
    for piece in finish_pieces(cells - 1, c1, o1, out_ref, wall_ref):
        piece()


def wall_kernel(
    ids_ref,
    patch_ref,
    point_ref,
    density_ref,
    weight_ref,
    out_ref,
    back_ref,
    s0,
    s1,
    r0,
    r1,
    w0,
    w1,
    o0,
    o1,
    a0,
    a1,
    c0,
    c1,
    feature_ref,
    p0,
    p1,
    pick_ref,
):
    cells = out_ref.shape[0]
    points = out_ref.shape[2]
    tiles = r0.shape[1] // lanes
    blocks = 2
    lane = lax.broadcasted_iota(jnp.int32, (8, lanes), 1)

    def prepare(j, center, r_ref, w_ref):
        parts = []
        for t in range(tiles):
            left, right = ids_ref[j, 2 * t], ids_ref[j, 2 * t + 1]
            one = pltpu.roll(patch_ref[left // 2], 64 * (left % 2), 1)
            two = pltpu.roll(patch_ref[right // 2], 64 * (1 - right % 2), 1)
            parts.append(jnp.where(lane < 64, one, two) - center)
        raw = jnp.concatenate(parts, axis=1)
        r_ref[...] = raw
        w_ref[...] = source_features(raw)

    def chunk(start, s_ref, r_ref, acc_ref, own_ref, back):
        acc = [[None] * blocks for _ in range(4)]
        own = [
            [own_ref[start + 8 * b : start + 8 * b + 8, k * lanes : k * lanes + lanes] for k in range(6)]
            for b in range(blocks)
        ]
        for c in range(tiles):
            cols = slice(c * lanes, c * lanes + lanes)
            src = source_rows(r_ref, cols)
            for b in range(blocks):
                top = start + 8 * b
                h = lax.rsqrt(s_ref[top : top + 8, cols])
                cube = h * h * h
                whole = h + cube
                m = s_ref[points + top : points + top + 8, cols] * cube
                n = s_ref[2 * points + top : 2 * points + top + 8, cols] * cube
                acc[3][b] = added(acc[3][b], m)
                back[c][3] = added(back[c][3], n)
                for k in range(3):
                    acc[k][b] = added(acc[k][b], whole * src[3 + k]) - m * src[k]
                    back[c][k] = added(back[c][k], whole * own[b][3 + k]) - n * own[b][k]
        for b in range(blocks):
            top = start + 8 * b
            for k in range(3):
                line = acc[k][b] + own[b][k] * acc[3][b]
                acc_ref[top : top + 8, k : k + 1] = jnp.sum(line, axis=1, keepdims=True)

    def give_back(j, r_ref, back):
        for c in range(tiles):
            rows = [jnp.sum(back[c][k], axis=0, keepdims=True) for k in range(4)]
            rows = jnp.concatenate(rows + [jnp.zeros((4, lanes), f32)], axis=0)
            term = rows + r_ref[:, c * lanes : c * lanes + lanes] * rows[3:4, :]
            for half in range(2):
                patch = ids_ref[j, 2 * c + half]
                odd = patch % 2
                moved = pltpu.roll(term, 64 * (odd if half == 0 else 1 - odd), 1)
                kept = jnp.where((lane >= 64) == (odd == 1), moved, 0.0)
                back_ref[patch // 2] += kept

    def step(j, r_ref, w_ref, own_ref, a_ref):
        center = prepare_own(j, point_ref, density_ref, weight_ref, feature_ref, own_ref, a_ref, 3)
        prepare(j, center, r_ref, w_ref)

    def spread_pieces(a_ref, p_ref):
        half = 3 * lanes

        def positions():
            p_ref[:, :half] = jnp.dot(a_ref[:points], pick_ref[:, :half], preferred_element_type=f32)

        def loads():
            p_ref[:, half:] = jnp.dot(a_ref[2 * points :], pick_ref[:, half:], preferred_element_type=f32)

        return [positions, loads]

    def stage(j, now, later, last):
        s_ref, r_ref, w_ref, own_ref, a_ref, acc_ref, p_ref = now
        next_s, next_r, next_w, next_own, next_a, next_acc, next_p = later
        side = finish_pieces(jnp.maximum(j - 1, 0), next_acc, next_own, out_ref, None)
        side += [lambda: step(last, next_r, next_w, next_own, next_a)]
        side += product_tiles(next_a, next_w, next_s) + spread_pieces(next_a, next_p)
        back = [[None] * 4 for _ in range(tiles)]
        main = [lambda t=t: chunk(t, s_ref, r_ref, acc_ref, p_ref, back) for t in range(0, points, 8 * blocks)]
        woven(main, side)
        give_back(j, r_ref, back)

    even = (s0, r0, w0, o0, a0, c0, p0)
    odd = (s1, r1, w1, o1, a1, c1, p1)
    back_ref[...] = jnp.zeros_like(back_ref)
    start_features(feature_ref)
    feature = lax.broadcasted_iota(jnp.int32, pick_ref.shape, 0)
    column = lax.broadcasted_iota(jnp.int32, pick_ref.shape, 1) // lanes
    hit = (feature < 24) & (feature % 8 == column % 3)
    pick_ref[...] = jnp.where(hit, jnp.where(column < 3, 1.0, -2.0), 0.0).astype(bf16)
    c0[...] = jnp.zeros_like(c0)
    c1[...] = jnp.zeros_like(c1)
    o1[...] = jnp.zeros_like(o1)
    step(0, r0, w0, o0, a0)
    for piece in product_tiles(a0, w0, s0) + spread_pieces(a0, p0):
        piece()

    def body(i, carry):
        j = 2 * i
        stage(j, even, odd, j + 1)
        stage(j + 1, odd, even, jnp.minimum(j + 2, cells - 1))
        return carry

    lax.fori_loop(0, cells // 2, body, 0)
    for piece in finish_pieces(cells - 1, c1, o1, out_ref, None):
        piece()


def scratch(points, kinds, tiles):
    wide = -(-points // lanes) * lanes
    pairs = [
        pltpu.VMEM((kinds * points, tiles * lanes), f32),
        pltpu.VMEM((8, tiles * lanes), f32),
        pltpu.VMEM((depth, tiles * lanes), bf16),
        pltpu.VMEM((8, wide), f32),
        pltpu.VMEM((kinds * points, depth), bf16),
        pltpu.VMEM((wide, lanes), f32),
    ]
    shapes = [shape for shape in pairs for _ in range(2)]
    shapes += [pltpu.VMEM((kinds * depth, wide), f32)]
    if kinds == 3:
        shapes += [pltpu.VMEM((points, 6 * lanes), f32)] * 2 + [pltpu.VMEM((depth, 6 * lanes), bf16)]
    return shapes


def local(
    cell_points,
    cell_density,
    cell_weights,
    near_device,
    near_slot,
    near_wall,
    wall_points,
    wall_density,
    wall_weights,
):
    wall_count = lax.axis_size("wall")
    wall_index = lax.axis_index("wall")
    cells, _, points = cell_points.shape
    patch_dev, _, patch_pts = wall_points.shape
    quarter = points // wall_count
    extra = quarter - lanes
    part = patch_pts // wall_count
    vmem = pl.BlockSpec(memory_space=pltpu.VMEM)
    smem = pl.BlockSpec(memory_space=pltpu.SMEM)
    params = pltpu.CompilerParams(vmem_limit_bytes=60 * 2**20)

    cell_load = cell_density * cell_weights[:, None, :]
    raw = jnp.concatenate([2.0 * cell_points, cell_load], axis=1)
    mine = lax.dynamic_slice_in_dim(raw, wall_index * quarter, quarter, 2)
    gap = jnp.zeros((cells, lanes - 6 * extra), f32)
    ends = [mine[:, q, lanes:] for q in range(6)]
    tail = jnp.concatenate([ends[0], gap] + ends[:0:-1], axis=1)[:, None, :]
    block = jnp.concatenate([mine[:, :, :lanes], tail, jnp.zeros((cells, 1, lanes), f32)], axis=1)
    groups = lax.axis_size("cell")
    copies = jnp.broadcast_to(block[None], (groups,) + block.shape).reshape(groups * cells, 8, lanes)
    gathered = lax.all_to_all(copies, "cell", split_axis=0, concat_axis=0, tiled=True)

    wall_raw = jnp.concatenate(
        [2.0 * wall_points, wall_density * wall_weights[:, None, :], jnp.zeros((patch_dev, 2, patch_pts), f32)],
        axis=1,
    )
    wall_raw = wall_raw.reshape(patch_dev // 2, 2, 8, wall_count, part).transpose(3, 0, 2, 1, 4)
    wall_raw = wall_raw.reshape(wall_count * (patch_dev // 2), 8, 2 * part)
    patches = lax.all_to_all(wall_raw, "wall", split_axis=0, concat_axis=0, tiled=True)

    tiles = near_wall.shape[1] * part // lanes
    wall_term, back = pl.pallas_call(
        wall_kernel,
        out_shape=(
            jax.ShapeDtypeStruct((cells, 3, points), f32),
            jax.ShapeDtypeStruct(patches.shape, f32),
        ),
        in_specs=[smem] + [vmem] * 4,
        out_specs=(vmem, vmem),
        scratch_shapes=scratch(points, 3, tiles),
        compiler_params=params,
        cost_estimate=pl.CostEstimate(flops=7 * 10**10, bytes_accessed=10**7, transcendentals=0),
        name="wall_pairs",
    )(near_wall, patches, cell_points, cell_density, cell_weights)

    near_ids = near_device * cells + near_slot
    tiles = near_device.shape[1] + 1
    total = pl.pallas_call(
        near_kernel,
        out_shape=jax.ShapeDtypeStruct((cells, 3, points), f32),
        in_specs=[smem] + [vmem] * 5,
        out_specs=vmem,
        scratch_shapes=scratch(points, 2, tiles),
        compiler_params=params,
        cost_estimate=pl.CostEstimate(flops=7 * 10**10, bytes_accessed=10**7, transcendentals=0),
        name="near_pairs",
    )(near_ids, gathered, cell_points, cell_density, cell_weights, wall_term)

    pairs = patch_dev // 2
    total = total.reshape(cells, 3, wall_count, quarter).transpose(2, 0, 1, 3)
    back = back[:, :3, :].reshape(wall_count, pairs, 3, lanes)
    both = jnp.concatenate(
        [total.reshape(wall_count, -1, lanes), back.reshape(wall_count, -1, lanes)], axis=1
    )
    both = lax.all_to_all(both, "wall", split_axis=0, concat_axis=0, tiled=True)
    cut = cells * 3 * quarter // lanes
    share = jnp.sum(both[:, :cut], axis=0).reshape(cells, 3, quarter)
    own = lax.dynamic_slice_in_dim(cell_density, wall_index * quarter, quarter, 2)
    velocity = 0.5 * own + two_stokes_factor * share
    back = both[:, cut:].reshape(wall_count, pairs, 3, 2, part).transpose(1, 3, 2, 0, 4)
    wall_velocity = 0.5 * wall_density + two_stokes_factor * back.reshape(patch_dev, 3, patch_pts)
    return (velocity, wall_velocity)


def solution(mesh):
    in_specs = (
        P("cell", None, None),
        P("cell", None, None),
        P("cell", None),
        P("cell", None),
        P("cell", None),
        P("cell", None),
        P(("cell", "wall"), None, None),
        P(("cell", "wall"), None, None),
        P(("cell", "wall"), None),
    )
    out_specs = (P("cell", None, "wall"), P(("cell", "wall"), None, None))
    return jax.shard_map(local, mesh=mesh, in_specs=in_specs, out_specs=out_specs, check_vma=False)
```

```python
import jax
import jax.numpy as jnp
from jax import lax
from jax.experimental import pallas as pl
from jax.experimental.pallas import tpu as pltpu
from jax.sharding import PartitionSpec as P

f32 = jnp.float32
bf16 = jnp.bfloat16
two_stokes_factor = 2.0 * 0.039788735772973836
levels = ((1, 1), (1, 2), (1, 3), (2, 1), (2, 2), (3, 1))
depth = 64
lanes = 128


def split3(x):
    first = x.astype(bf16).astype(f32)
    rest = x - first
    second = rest.astype(bf16).astype(f32)
    return first, second, rest - second


def source_features(raw):
    y = [raw[i : i + 1, :] for i in range(3)]
    g = [raw[i : i + 1, :] for i in range(3, 6)]
    square = y[0] * y[0] + y[1] * y[1] + y[2] * y[2] + 1.0
    dot = g[0] * y[0] + g[1] * y[1] + g[2] * y[2]
    rows = jnp.concatenate(
        [-2.0 * y[0], -2.0 * y[1], -2.0 * y[2], square, g[0], g[1], g[2], -dot], axis=0
    )
    parts = split3(rows)
    one = jnp.ones_like(rows)
    stack = [parts[p - 1] for p, _ in levels] + [one, jnp.zeros_like(rows)]
    return jnp.concatenate(stack, axis=0).astype(bf16)


def prepare_own(j, point_ref, density_ref, weight_ref, feature_ref, own_ref, a_ref, kinds):
    points = point_ref.shape[2]
    x = 2.0 * point_ref[j]
    center = jnp.sum(x, axis=1, keepdims=True) * (1.0 / points)
    x = x - center
    load = density_ref[j] * weight_ref[pl.ds(j, 1), :]
    own_ref[0:3, :points] = x
    own_ref[3:6, :points] = load
    xs = split3(x)
    squares = split3(jnp.sum(x * x, axis=0, keepdims=True))
    for i, (_, q) in enumerate(levels):
        feature_ref[8 * i : 8 * i + 3, :points] = xs[q - 1]
        feature_ref[depth + 8 * i + 4 : depth + 8 * i + 7, :points] = xs[q - 1]
    for i in range(3):
        feature_ref[48 + i : 49 + i, :points] = squares[i]
    if kinds == 3:
        ls = split3(-0.5 * load)
        dots = split3(-jnp.sum(x * load, axis=0, keepdims=True))
        for i, (_, q) in enumerate(levels):
            feature_ref[2 * depth + 8 * i : 2 * depth + 8 * i + 3, :points] = ls[q - 1]
        for i in range(3):
            feature_ref[2 * depth + 48 + i : 2 * depth + 49 + i, :points] = dots[i]
    for kind in range(kinds):
        turned = feature_ref[kind * depth : kind * depth + depth, :].T
        a_ref[kind * points : kind * points + points, :] = turned[:points].astype(bf16)
    return jnp.concatenate([jnp.broadcast_to(center, (3, lanes)), jnp.zeros((5, lanes), f32)], axis=0)


def start_features(feature_ref):
    feature_ref[...] = jnp.zeros_like(feature_ref)
    one = jnp.ones((1, feature_ref.shape[1]), f32)
    for i, (_, q) in enumerate(levels):
        if q == 1:
            feature_ref[8 * i + 3 : 8 * i + 4, :] = one
            feature_ref[depth + 8 * i + 7 : depth + 8 * i + 8, :] = one


def product_tiles(a_ref, w_ref, s_ref):
    n = w_ref.shape[1]

    def tile(c):
        e = min(n, c + 256)
        s_ref[:, c:e] = jnp.dot(a_ref[...], w_ref[:, c:e], preferred_element_type=f32)

    return [lambda c=c: tile(c) for c in range(0, n, 256)]


def source_rows(r_ref, cols):
    return [jnp.broadcast_to(r_ref[i : i + 1, cols], (8, lanes)) for i in range(6)]


def added(total, term):
    return term if total is None else total + term


def woven(main, side):
    done = 0
    for i, piece in enumerate(main):
        while done < len(side) and done * len(main) <= i * len(side):
            side[done]()
            done += 1
        piece()
    for piece in side[done:]:
        piece()


def finish_pieces(j, acc_ref, own_ref, out_ref, more_ref):
    points = out_ref.shape[2]

    def turn():
        turned = acc_ref[...].T
        if more_ref is None:
            out_ref[j] = turned[0:3, :points]
        else:
            out_ref[j] = turned[0:3, :points] + own_ref[0:3, :points] * turned[3:4, :points] + more_ref[j]

    return [turn]


def near_kernel(
    ids_ref,
    gathered_ref,
    point_ref,
    density_ref,
    weight_ref,
    wall_ref,
    out_ref,
    s0,
    s1,
    r0,
    r1,
    w0,
    w1,
    o0,
    o1,
    a0,
    a1,
    c0,
    c1,
    feature_ref,
):
    cells = out_ref.shape[0]
    points = out_ref.shape[2]
    tiles = r0.shape[1] // lanes
    blocks = 4

    def prepare(j, center, r_ref, w_ref):
        lane = lax.broadcasted_iota(jnp.int32, (8, lanes), 1)
        tail = jnp.zeros((8, lanes), f32)
        parts = []
        for k in range(8):
            block = gathered_ref[ids_ref[j, k]]
            parts.append(block - center)
            last = jnp.broadcast_to(block[6:7, :], (8, lanes))
            last = pltpu.roll(last, 8 * k, 1, stride=8, stride_axis=0)
            tail = jnp.where((lane >= 8 * k) & (lane < 8 * k + 8), last, tail)
        parts.append(jnp.where(lane < 64, tail - center, 0.0))
        raw = jnp.concatenate(parts, axis=1)
        r_ref[...] = raw
        w_ref[...] = source_features(raw)

    def chunk(start, s_ref, r_ref, acc_ref):
        acc = [[None] * blocks for _ in range(4)]
        for c in range(tiles):
            cols = slice(c * lanes, c * lanes + lanes)
            src = source_rows(r_ref, cols)
            for b in range(blocks):
                top = start + 8 * b
                h = lax.rsqrt(s_ref[top : top + 8, cols])
                cube = h * h * h
                whole = h + cube
                m = s_ref[points + top : points + top + 8, cols] * cube
                acc[3][b] = added(acc[3][b], m)
                for k in range(3):
                    acc[k][b] = added(acc[k][b], whole * src[3 + k]) - m * src[k]
        for b in range(blocks):
            top = start + 8 * b
            for k in range(4):
                acc_ref[top : top + 8, k : k + 1] = jnp.sum(acc[k][b], axis=1, keepdims=True)

    def step(j, r_ref, w_ref, own_ref, a_ref):
        center = prepare_own(j, point_ref, density_ref, weight_ref, feature_ref, own_ref, a_ref, 2)
        prepare(j, center, r_ref, w_ref)

    def stage(j, now, later, last):
        s_ref, r_ref, w_ref, own_ref, a_ref, acc_ref = now
        next_s, next_r, next_w, next_own, next_a, next_acc = later
        side = finish_pieces(jnp.maximum(j - 1, 0), next_acc, next_own, out_ref, wall_ref)
        side += [lambda: step(last, next_r, next_w, next_own, next_a)]
        side += product_tiles(next_a, next_w, next_s)
        main = [lambda t=t: chunk(t, s_ref, r_ref, acc_ref) for t in range(0, points, 8 * blocks)]
        woven(main, side)

    even = (s0, r0, w0, o0, a0, c0)
    odd = (s1, r1, w1, o1, a1, c1)
    start_features(feature_ref)
    c0[...] = jnp.zeros_like(c0)
    c1[...] = jnp.zeros_like(c1)
    o1[...] = jnp.zeros_like(o1)
    step(0, r0, w0, o0, a0)
    for piece in product_tiles(a0, w0, s0):
        piece()

    def body(i, carry):
        j = 2 * i
        stage(j, even, odd, j + 1)
        stage(j + 1, odd, even, jnp.minimum(j + 2, cells - 1))
        return carry

    lax.fori_loop(0, cells // 2, body, 0)
    for piece in finish_pieces(cells - 1, c1, o1, out_ref, wall_ref):
        piece()


def wall_kernel(
    ids_ref,
    patch_ref,
    point_ref,
    density_ref,
    weight_ref,
    out_ref,
    back_ref,
    s0,
    s1,
    r0,
    r1,
    w0,
    w1,
    o0,
    o1,
    a0,
    a1,
    c0,
    c1,
    feature_ref,
    p0,
    p1,
    pick_ref,
):
    cells = out_ref.shape[0]
    points = out_ref.shape[2]
    tiles = r0.shape[1] // lanes
    blocks = 2
    lane = lax.broadcasted_iota(jnp.int32, (8, lanes), 1)

    def prepare(j, center, r_ref, w_ref):
        parts = []
        for t in range(tiles):
            left, right = ids_ref[j, 2 * t], ids_ref[j, 2 * t + 1]
            one = pltpu.roll(patch_ref[left // 2], 64 * (left % 2), 1)
            two = pltpu.roll(patch_ref[right // 2], 64 * (1 - right % 2), 1)
            parts.append(jnp.where(lane < 64, one, two) - center)
        raw = jnp.concatenate(parts, axis=1)
        r_ref[...] = raw
        w_ref[...] = source_features(raw)

    def chunk(start, s_ref, r_ref, acc_ref, own_ref, back):
        acc = [[None] * blocks for _ in range(4)]
        own = [
            [own_ref[start + 8 * b : start + 8 * b + 8, k * lanes : k * lanes + lanes] for k in range(6)]
            for b in range(blocks)
        ]
        for c in range(tiles):
            cols = slice(c * lanes, c * lanes + lanes)
            src = source_rows(r_ref, cols)
            for b in range(blocks):
                top = start + 8 * b
                h = lax.rsqrt(s_ref[top : top + 8, cols])
                cube = h * h * h
                whole = h + cube
                m = s_ref[points + top : points + top + 8, cols] * cube
                n = s_ref[2 * points + top : 2 * points + top + 8, cols] * cube
                acc[3][b] = added(acc[3][b], m)
                back[c][3] = added(back[c][3], n)
                for k in range(3):
                    acc[k][b] = added(acc[k][b], whole * src[3 + k]) - m * src[k]
                    back[c][k] = added(back[c][k], whole * own[b][3 + k]) - n * own[b][k]
        for b in range(blocks):
            top = start + 8 * b
            for k in range(3):
                line = acc[k][b] + own[b][k] * acc[3][b]
                acc_ref[top : top + 8, k : k + 1] = jnp.sum(line, axis=1, keepdims=True)

    def give_back(j, r_ref, back):
        for c in range(tiles):
            rows = [jnp.sum(back[c][k], axis=0, keepdims=True) for k in range(4)]
            rows = jnp.concatenate(rows + [jnp.zeros((4, lanes), f32)], axis=0)
            term = rows + r_ref[:, c * lanes : c * lanes + lanes] * rows[3:4, :]
            for half in range(2):
                patch = ids_ref[j, 2 * c + half]
                odd = patch % 2
                moved = pltpu.roll(term, 64 * (odd if half == 0 else 1 - odd), 1)
                kept = jnp.where((lane >= 64) == (odd == 1), moved, 0.0)
                back_ref[patch // 2] += kept

    def step(j, r_ref, w_ref, own_ref, a_ref):
        center = prepare_own(j, point_ref, density_ref, weight_ref, feature_ref, own_ref, a_ref, 3)
        prepare(j, center, r_ref, w_ref)

    def spread_pieces(a_ref, p_ref):
        half = 3 * lanes

        def positions():
            p_ref[:, :half] = jnp.dot(a_ref[:points], pick_ref[:, :half], preferred_element_type=f32)

        def loads():
            p_ref[:, half:] = jnp.dot(a_ref[2 * points :], pick_ref[:, half:], preferred_element_type=f32)

        return [positions, loads]

    def stage(j, now, later, last):
        s_ref, r_ref, w_ref, own_ref, a_ref, acc_ref, p_ref = now
        next_s, next_r, next_w, next_own, next_a, next_acc, next_p = later
        side = finish_pieces(jnp.maximum(j - 1, 0), next_acc, next_own, out_ref, None)
        side += [lambda: step(last, next_r, next_w, next_own, next_a)]
        side += product_tiles(next_a, next_w, next_s) + spread_pieces(next_a, next_p)
        back = [[None] * 4 for _ in range(tiles)]
        main = [lambda t=t: chunk(t, s_ref, r_ref, acc_ref, p_ref, back) for t in range(0, points, 8 * blocks)]
        woven(main, side)
        give_back(j, r_ref, back)

    even = (s0, r0, w0, o0, a0, c0, p0)
    odd = (s1, r1, w1, o1, a1, c1, p1)
    back_ref[...] = jnp.zeros_like(back_ref)
    start_features(feature_ref)
    feature = lax.broadcasted_iota(jnp.int32, pick_ref.shape, 0)
    column = lax.broadcasted_iota(jnp.int32, pick_ref.shape, 1) // lanes
    hit = (feature < 24) & (feature % 8 == column % 3)
    pick_ref[...] = jnp.where(hit, jnp.where(column < 3, 1.0, -2.0), 0.0).astype(bf16)
    c0[...] = jnp.zeros_like(c0)
    c1[...] = jnp.zeros_like(c1)
    o1[...] = jnp.zeros_like(o1)
    step(0, r0, w0, o0, a0)
    for piece in product_tiles(a0, w0, s0) + spread_pieces(a0, p0):
        piece()

    def body(i, carry):
        j = 2 * i
        stage(j, even, odd, j + 1)
        stage(j + 1, odd, even, jnp.minimum(j + 2, cells - 1))
        return carry

    lax.fori_loop(0, cells // 2, body, 0)
    for piece in finish_pieces(cells - 1, c1, o1, out_ref, None):
        piece()


def exchange_kernel(count, x_ref, out_ref, sent, received, kept):
    me = lax.axis_index("wall")
    barrier = pltpu.get_barrier_semaphore()
    for d in range(1, count):
        peer = lax.rem(me + d, count)
        pl.semaphore_signal(barrier, inc=1, device_id={"wall": peer}, device_id_type=pl.DeviceIdType.MESH)
    own = pltpu.make_async_copy(x_ref.at[me], out_ref.at[me], kept)
    own.start()
    pl.semaphore_wait(barrier, count - 1)
    copies = []
    for d in range(1, count):
        peer = lax.rem(me + d, count)
        copy = pltpu.make_async_remote_copy(
            src_ref=x_ref.at[peer],
            dst_ref=out_ref.at[me],
            send_sem=sent.at[d - 1],
            recv_sem=received.at[d - 1],
            device_id={"wall": peer},
            device_id_type=pl.DeviceIdType.MESH,
        )
        copy.start()
        copies.append(copy)
    own.wait()
    for copy in copies:
        copy.wait()


def exchange(x, number):
    count = x.shape[0]

    def kernel(*refs):
        exchange_kernel(count, *refs)

    vmem = pl.BlockSpec(memory_space=pltpu.VMEM)
    return pl.pallas_call(
        kernel,
        out_shape=jax.ShapeDtypeStruct(x.shape, f32),
        in_specs=[vmem],
        out_specs=vmem,
        scratch_shapes=[
            pltpu.SemaphoreType.DMA((count - 1,)),
            pltpu.SemaphoreType.DMA((count - 1,)),
            pltpu.SemaphoreType.DMA,
        ],
        compiler_params=pltpu.CompilerParams(
            collective_id=number, has_side_effects=True, vmem_limit_bytes=16 * 2**20
        ),
        cost_estimate=pl.CostEstimate(flops=5 * 10**9, bytes_accessed=10**6, transcendentals=0),
        name="exchange_%d" % number,
    )(x)


def scratch(points, kinds, tiles):
    wide = -(-points // lanes) * lanes
    pairs = [
        pltpu.VMEM((kinds * points, tiles * lanes), f32),
        pltpu.VMEM((8, tiles * lanes), f32),
        pltpu.VMEM((depth, tiles * lanes), bf16),
        pltpu.VMEM((8, wide), f32),
        pltpu.VMEM((kinds * points, depth), bf16),
        pltpu.VMEM((wide, lanes), f32),
    ]
    shapes = [shape for shape in pairs for _ in range(2)]
    shapes += [pltpu.VMEM((kinds * depth, wide), f32)]
    if kinds == 3:
        shapes += [pltpu.VMEM((points, 6 * lanes), f32)] * 2 + [pltpu.VMEM((depth, 6 * lanes), bf16)]
    return shapes


def local(
    cell_points,
    cell_density,
    cell_weights,
    near_device,
    near_slot,
    near_wall,
    wall_points,
    wall_density,
    wall_weights,
):
    wall_count = lax.axis_size("wall")
    wall_index = lax.axis_index("wall")
    cells, _, points = cell_points.shape
    patch_dev, _, patch_pts = wall_points.shape
    quarter = points // wall_count
    extra = quarter - lanes
    part = patch_pts // wall_count
    vmem = pl.BlockSpec(memory_space=pltpu.VMEM)
    smem = pl.BlockSpec(memory_space=pltpu.SMEM)
    params = pltpu.CompilerParams(vmem_limit_bytes=60 * 2**20)

    cell_load = cell_density * cell_weights[:, None, :]
    raw = jnp.concatenate([2.0 * cell_points, cell_load], axis=1)
    mine = lax.dynamic_slice_in_dim(raw, wall_index * quarter, quarter, 2)
    gap = jnp.zeros((cells, lanes - 6 * extra), f32)
    ends = [mine[:, q, lanes:] for q in range(6)]
    tail = jnp.concatenate([ends[0], gap] + ends[:0:-1], axis=1)[:, None, :]
    block = jnp.concatenate([mine[:, :, :lanes], tail, jnp.zeros((cells, 1, lanes), f32)], axis=1)
    groups = lax.axis_size("cell")
    copies = jnp.broadcast_to(block[None], (groups,) + block.shape).reshape(groups * cells, 8, lanes)
    gathered = lax.all_to_all(copies, "cell", split_axis=0, concat_axis=0, tiled=True)

    wall_raw = jnp.concatenate(
        [2.0 * wall_points, wall_density * wall_weights[:, None, :], jnp.zeros((patch_dev, 2, patch_pts), f32)],
        axis=1,
    )
    wall_raw = wall_raw.reshape(patch_dev // 2, 2, 8, wall_count, part).transpose(3, 0, 2, 1, 4)
    wall_raw = wall_raw.reshape(wall_count, (patch_dev // 2) * 8, 2 * part)
    patches = exchange(wall_raw, 0).reshape(wall_count * (patch_dev // 2), 8, 2 * part)

    tiles = near_wall.shape[1] * part // lanes
    wall_term, back = pl.pallas_call(
        wall_kernel,
        out_shape=(
            jax.ShapeDtypeStruct((cells, 3, points), f32),
            jax.ShapeDtypeStruct(patches.shape, f32),
        ),
        in_specs=[smem] + [vmem] * 4,
        out_specs=(vmem, vmem),
        scratch_shapes=scratch(points, 3, tiles),
        compiler_params=params,
        cost_estimate=pl.CostEstimate(flops=7 * 10**10, bytes_accessed=10**7, transcendentals=0),
        name="wall_pairs",
    )(near_wall, patches, cell_points, cell_density, cell_weights)

    near_ids = near_device * cells + near_slot
    tiles = near_device.shape[1] + 1
    total = pl.pallas_call(
        near_kernel,
        out_shape=jax.ShapeDtypeStruct((cells, 3, points), f32),
        in_specs=[smem] + [vmem] * 5,
        out_specs=vmem,
        scratch_shapes=scratch(points, 2, tiles),
        compiler_params=params,
        cost_estimate=pl.CostEstimate(flops=7 * 10**10, bytes_accessed=10**7, transcendentals=0),
        name="near_pairs",
    )(near_ids, gathered, cell_points, cell_density, cell_weights, wall_term)

    pairs = patch_dev // 2
    total = total.reshape(cells, 3, wall_count, quarter).transpose(2, 0, 1, 3)
    back = back[:, :3, :].reshape(wall_count, pairs, 3, lanes)
    both = jnp.concatenate(
        [total.reshape(wall_count, -1, lanes), back.reshape(wall_count, -1, lanes)], axis=1
    )
    both = exchange(both, 1)
    cut = cells * 3 * quarter // lanes
    share = jnp.sum(both[:, :cut], axis=0).reshape(cells, 3, quarter)
    own = lax.dynamic_slice_in_dim(cell_density, wall_index * quarter, quarter, 2)
    velocity = 0.5 * own + two_stokes_factor * share
    back = both[:, cut:].reshape(wall_count, pairs, 3, 2, part).transpose(1, 3, 2, 0, 4)
    wall_velocity = 0.5 * wall_density + two_stokes_factor * back.reshape(patch_dev, 3, patch_pts)
    return (velocity, wall_velocity)


def solution(mesh):
    in_specs = (
        P("cell", None, None),
        P("cell", None, None),
        P("cell", None),
        P("cell", None),
        P("cell", None),
        P("cell", None),
        P(("cell", "wall"), None, None),
        P(("cell", "wall"), None, None),
        P(("cell", "wall"), None),
    )
    out_specs = (P("cell", None, "wall"), P(("cell", "wall"), None, None))
    return jax.shard_map(local, mesh=mesh, in_specs=in_specs, out_specs=out_specs, check_vma=False)
```

```python
import jax
import jax.numpy as jnp
from jax import lax
from jax.experimental import pallas as pl
from jax.experimental.pallas import tpu as pltpu
from jax.sharding import PartitionSpec as P

f32 = jnp.float32
bf16 = jnp.bfloat16
two_stokes_factor = 2.0 * 0.039788735772973836
levels = ((1, 1), (1, 2), (1, 3), (2, 1), (2, 2), (3, 1))
depth = 64
lanes = 128


def split3(x):
    first = x.astype(bf16).astype(f32)
    rest = x - first
    second = rest.astype(bf16).astype(f32)
    return first, second, rest - second


def source_features(raw):
    y = [raw[i : i + 1, :] for i in range(3)]
    g = [raw[i : i + 1, :] for i in range(3, 6)]
    square = y[0] * y[0] + y[1] * y[1] + y[2] * y[2] + 1.0
    dot = g[0] * y[0] + g[1] * y[1] + g[2] * y[2]
    rows = jnp.concatenate(
        [-2.0 * y[0], -2.0 * y[1], -2.0 * y[2], square, g[0], g[1], g[2], -dot], axis=0
    )
    parts = split3(rows)
    one = jnp.ones_like(rows)
    stack = [parts[p - 1] for p, _ in levels] + [one, jnp.zeros_like(rows)]
    return jnp.concatenate(stack, axis=0).astype(bf16)


def prepare_own(j, point_ref, density_ref, weight_ref, feature_ref, own_ref, a_ref, kinds):
    points = point_ref.shape[2]
    x = 2.0 * point_ref[j]
    center = jnp.sum(x, axis=1, keepdims=True) * (1.0 / points)
    x = x - center
    load = density_ref[j] * weight_ref[pl.ds(j, 1), :]
    own_ref[0:3, :points] = x
    own_ref[3:6, :points] = load
    xs = split3(x)
    squares = split3(jnp.sum(x * x, axis=0, keepdims=True))
    for i, (_, q) in enumerate(levels):
        feature_ref[8 * i : 8 * i + 3, :points] = xs[q - 1]
        feature_ref[depth + 8 * i + 4 : depth + 8 * i + 7, :points] = xs[q - 1]
    for i in range(3):
        feature_ref[48 + i : 49 + i, :points] = squares[i]
    if kinds == 3:
        ls = split3(-0.5 * load)
        dots = split3(-jnp.sum(x * load, axis=0, keepdims=True))
        for i, (_, q) in enumerate(levels):
            feature_ref[2 * depth + 8 * i : 2 * depth + 8 * i + 3, :points] = ls[q - 1]
        for i in range(3):
            feature_ref[2 * depth + 48 + i : 2 * depth + 49 + i, :points] = dots[i]
    for kind in range(kinds):
        turned = feature_ref[kind * depth : kind * depth + depth, :].T
        a_ref[kind * points : kind * points + points, :] = turned[:points].astype(bf16)
    return jnp.concatenate([jnp.broadcast_to(center, (3, lanes)), jnp.zeros((5, lanes), f32)], axis=0)


def start_features(feature_ref):
    feature_ref[...] = jnp.zeros_like(feature_ref)
    one = jnp.ones((1, feature_ref.shape[1]), f32)
    for i, (_, q) in enumerate(levels):
        if q == 1:
            feature_ref[8 * i + 3 : 8 * i + 4, :] = one
            feature_ref[depth + 8 * i + 7 : depth + 8 * i + 8, :] = one


def product_tiles(a_ref, w_ref, s_ref):
    n = w_ref.shape[1]

    def tile(c):
        e = min(n, c + 256)
        s_ref[:, c:e] = jnp.dot(a_ref[...], w_ref[:, c:e], preferred_element_type=f32)

    return [lambda c=c: tile(c) for c in range(0, n, 256)]


def source_rows(r_ref, cols):
    return [jnp.broadcast_to(r_ref[i : i + 1, cols], (8, lanes)) for i in range(6)]


def added(total, term):
    return term if total is None else total + term


def woven(main, side):
    done = 0
    for i, piece in enumerate(main):
        while done < len(side) and done * len(main) <= i * len(side):
            side[done]()
            done += 1
        piece()
    for piece in side[done:]:
        piece()


def finish_pieces(j, acc_ref, own_ref, out_ref, more_ref):
    points = out_ref.shape[2]

    def turn():
        turned = acc_ref[...].T
        if more_ref is None:
            out_ref[j] = turned[0:3, :points]
        else:
            out_ref[j] = turned[0:3, :points] + own_ref[0:3, :points] * turned[3:4, :points] + more_ref[j]

    return [turn]


def near_kernel(
    ids_ref,
    gathered_ref,
    point_ref,
    density_ref,
    weight_ref,
    wall_ref,
    out_ref,
    s0,
    s1,
    r0,
    r1,
    w0,
    w1,
    o0,
    o1,
    a0,
    a1,
    c0,
    c1,
    feature_ref,
):
    cells = out_ref.shape[0]
    points = out_ref.shape[2]
    tiles = r0.shape[1] // lanes
    blocks = 4

    def prepare(j, center, r_ref, w_ref):
        lane = lax.broadcasted_iota(jnp.int32, (8, lanes), 1)
        tail = jnp.zeros((8, lanes), f32)
        parts = []
        for k in range(8):
            block = gathered_ref[ids_ref[j, k]]
            parts.append(block - center)
            last = jnp.broadcast_to(block[6:7, :], (8, lanes))
            last = pltpu.roll(last, 8 * k, 1, stride=8, stride_axis=0)
            tail = jnp.where((lane >= 8 * k) & (lane < 8 * k + 8), last, tail)
        parts.append(jnp.where(lane < 64, tail - center, 0.0))
        raw = jnp.concatenate(parts, axis=1)
        r_ref[...] = jnp.concatenate([-raw[0:3], raw[3:8]], axis=0)
        w_ref[...] = source_features(raw)

    def chunk(start, s_ref, r_ref, acc_ref):
        acc = [[None] * blocks for _ in range(4)]
        for c in range(tiles):
            cols = slice(c * lanes, c * lanes + lanes)
            src = source_rows(r_ref, cols)
            for b in range(blocks):
                top = start + 8 * b
                h = lax.rsqrt(s_ref[top : top + 8, cols])
                cube = h * h * h
                whole = h + cube
                m = s_ref[points + top : points + top + 8, cols] * cube
                acc[3][b] = added(acc[3][b], m)
                for k in range(3):
                    acc[k][b] = added(acc[k][b], whole * src[3 + k]) + m * src[k]
        for b in range(blocks):
            top = start + 8 * b
            for k in range(4):
                acc_ref[top : top + 8, k : k + 1] = jnp.sum(acc[k][b], axis=1, keepdims=True)

    def step(j, r_ref, w_ref, own_ref, a_ref):
        center = prepare_own(j, point_ref, density_ref, weight_ref, feature_ref, own_ref, a_ref, 2)
        prepare(j, center, r_ref, w_ref)

    def stage(j, now, later, last):
        s_ref, r_ref, w_ref, own_ref, a_ref, acc_ref = now
        next_s, next_r, next_w, next_own, next_a, next_acc = later
        side = finish_pieces(jnp.maximum(j - 1, 0), next_acc, next_own, out_ref, wall_ref)
        side += [lambda: step(last, next_r, next_w, next_own, next_a)]
        side += product_tiles(next_a, next_w, next_s)
        main = [lambda t=t: chunk(t, s_ref, r_ref, acc_ref) for t in range(0, points, 8 * blocks)]
        woven(main, side)

    even = (s0, r0, w0, o0, a0, c0)
    odd = (s1, r1, w1, o1, a1, c1)
    start_features(feature_ref)
    c0[...] = jnp.zeros_like(c0)
    c1[...] = jnp.zeros_like(c1)
    o1[...] = jnp.zeros_like(o1)
    step(0, r0, w0, o0, a0)
    for piece in product_tiles(a0, w0, s0):
        piece()

    def body(i, carry):
        j = 2 * i
        stage(j, even, odd, j + 1)
        stage(j + 1, odd, even, jnp.minimum(j + 2, cells - 1))
        return carry

    lax.fori_loop(0, cells // 2, body, 0)
    for piece in finish_pieces(cells - 1, c1, o1, out_ref, wall_ref):
        piece()


def wall_kernel(
    ids_ref,
    patch_ref,
    point_ref,
    density_ref,
    weight_ref,
    out_ref,
    back_ref,
    s0,
    s1,
    r0,
    r1,
    w0,
    w1,
    o0,
    o1,
    a0,
    a1,
    c0,
    c1,
    feature_ref,
    p0,
    p1,
    pick_ref,
):
    cells = out_ref.shape[0]
    points = out_ref.shape[2]
    tiles = r0.shape[1] // lanes
    blocks = 2
    lane = lax.broadcasted_iota(jnp.int32, (8, lanes), 1)

    def prepare(j, center, r_ref, w_ref):
        parts = []
        for t in range(tiles):
            left, right = ids_ref[j, 2 * t], ids_ref[j, 2 * t + 1]
            one = pltpu.roll(patch_ref[left // 2], 64 * (left % 2), 1)
            two = pltpu.roll(patch_ref[right // 2], 64 * (1 - right % 2), 1)
            parts.append(jnp.where(lane < 64, one, two) - center)
        raw = jnp.concatenate(parts, axis=1)
        r_ref[...] = jnp.concatenate([-raw[0:3], raw[3:8]], axis=0)
        w_ref[...] = source_features(raw)

    def chunk(start, s_ref, r_ref, acc_ref, own_ref, back):
        acc = [[None] * blocks for _ in range(4)]
        own = [
            [own_ref[start + 8 * b : start + 8 * b + 8, k * lanes : k * lanes + lanes] for k in range(6)]
            for b in range(blocks)
        ]
        for c in range(tiles):
            cols = slice(c * lanes, c * lanes + lanes)
            src = source_rows(r_ref, cols)
            for b in range(blocks):
                top = start + 8 * b
                h = lax.rsqrt(s_ref[top : top + 8, cols])
                cube = h * h * h
                whole = h + cube
                m = s_ref[points + top : points + top + 8, cols] * cube
                n = s_ref[2 * points + top : 2 * points + top + 8, cols] * cube
                acc[3][b] = added(acc[3][b], m)
                back[c][3] = added(back[c][3], n)
                for k in range(3):
                    acc[k][b] = added(acc[k][b], whole * src[3 + k]) + m * src[k]
                    back[c][k] = added(back[c][k], whole * own[b][3 + k]) + n * own[b][k]
        for b in range(blocks):
            top = start + 8 * b
            for k in range(3):
                line = acc[k][b] - own[b][k] * acc[3][b]
                acc_ref[top : top + 8, k : k + 1] = jnp.sum(line, axis=1, keepdims=True)

    def give_back(j, r_ref, back):
        for c in range(tiles):
            rows = [jnp.sum(back[c][k], axis=0, keepdims=True) for k in range(4)]
            rows = jnp.concatenate(rows + [jnp.zeros((4, lanes), f32)], axis=0)
            term = rows - r_ref[:, c * lanes : c * lanes + lanes] * rows[3:4, :]
            for half in range(2):
                patch = ids_ref[j, 2 * c + half]
                odd = patch % 2
                moved = pltpu.roll(term, 64 * (odd if half == 0 else 1 - odd), 1)
                kept = jnp.where((lane >= 64) == (odd == 1), moved, 0.0)
                back_ref[patch // 2] += kept

    def step(j, r_ref, w_ref, own_ref, a_ref):
        center = prepare_own(j, point_ref, density_ref, weight_ref, feature_ref, own_ref, a_ref, 3)
        prepare(j, center, r_ref, w_ref)

    def spread_pieces(a_ref, p_ref):
        half = 3 * lanes

        def positions():
            p_ref[:, :half] = jnp.dot(a_ref[:points], pick_ref[:, :half], preferred_element_type=f32)

        def loads():
            p_ref[:, half:] = jnp.dot(a_ref[2 * points :], pick_ref[:, half:], preferred_element_type=f32)

        return [positions, loads]

    def stage(j, now, later, last):
        s_ref, r_ref, w_ref, own_ref, a_ref, acc_ref, p_ref = now
        next_s, next_r, next_w, next_own, next_a, next_acc, next_p = later
        side = finish_pieces(jnp.maximum(j - 1, 0), next_acc, next_own, out_ref, None)
        side += [lambda: step(last, next_r, next_w, next_own, next_a)]
        side += product_tiles(next_a, next_w, next_s) + spread_pieces(next_a, next_p)
        back = [[None] * 4 for _ in range(tiles)]
        main = [lambda t=t: chunk(t, s_ref, r_ref, acc_ref, p_ref, back) for t in range(0, points, 8 * blocks)]
        woven(main, side)
        give_back(j, r_ref, back)

    even = (s0, r0, w0, o0, a0, c0, p0)
    odd = (s1, r1, w1, o1, a1, c1, p1)
    back_ref[...] = jnp.zeros_like(back_ref)
    start_features(feature_ref)
    feature = lax.broadcasted_iota(jnp.int32, pick_ref.shape, 0)
    column = lax.broadcasted_iota(jnp.int32, pick_ref.shape, 1) // lanes
    hit = (feature < 24) & (feature % 8 == column % 3)
    pick_ref[...] = jnp.where(hit, jnp.where(column < 3, -1.0, -2.0), 0.0).astype(bf16)
    c0[...] = jnp.zeros_like(c0)
    c1[...] = jnp.zeros_like(c1)
    o1[...] = jnp.zeros_like(o1)
    step(0, r0, w0, o0, a0)
    for piece in product_tiles(a0, w0, s0) + spread_pieces(a0, p0):
        piece()

    def body(i, carry):
        j = 2 * i
        stage(j, even, odd, j + 1)
        stage(j + 1, odd, even, jnp.minimum(j + 2, cells - 1))
        return carry

    lax.fori_loop(0, cells // 2, body, 0)
    for piece in finish_pieces(cells - 1, c1, o1, out_ref, None):
        piece()


def exchange_kernel(count, x_ref, out_ref, sent, received, kept):
    me = lax.axis_index("wall")
    barrier = pltpu.get_barrier_semaphore()
    for d in range(1, count):
        peer = lax.rem(me + d, count)
        pl.semaphore_signal(barrier, inc=1, device_id={"wall": peer}, device_id_type=pl.DeviceIdType.MESH)
    own = pltpu.make_async_copy(x_ref.at[me], out_ref.at[me], kept)
    own.start()
    pl.semaphore_wait(barrier, count - 1)
    copies = []
    for d in range(1, count):
        peer = lax.rem(me + d, count)
        copy = pltpu.make_async_remote_copy(
            src_ref=x_ref.at[peer],
            dst_ref=out_ref.at[me],
            send_sem=sent.at[d - 1],
            recv_sem=received.at[d - 1],
            device_id={"wall": peer},
            device_id_type=pl.DeviceIdType.MESH,
        )
        copy.start()
        copies.append(copy)
    own.wait()
    for copy in copies:
        copy.wait()


def exchange(x, number):
    count = x.shape[0]

    def kernel(*refs):
        exchange_kernel(count, *refs)

    vmem = pl.BlockSpec(memory_space=pltpu.VMEM)
    return pl.pallas_call(
        kernel,
        out_shape=jax.ShapeDtypeStruct(x.shape, f32),
        in_specs=[vmem],
        out_specs=vmem,
        scratch_shapes=[
            pltpu.SemaphoreType.DMA((count - 1,)),
            pltpu.SemaphoreType.DMA((count - 1,)),
            pltpu.SemaphoreType.DMA,
        ],
        compiler_params=pltpu.CompilerParams(
            collective_id=number, has_side_effects=True, vmem_limit_bytes=16 * 2**20
        ),
        cost_estimate=pl.CostEstimate(flops=5 * 10**9, bytes_accessed=10**6, transcendentals=0),
        name="exchange_%d" % number,
    )(x)


def scratch(points, kinds, tiles):
    wide = -(-points // lanes) * lanes
    pairs = [
        pltpu.VMEM((kinds * points, tiles * lanes), f32),
        pltpu.VMEM((8, tiles * lanes), f32),
        pltpu.VMEM((depth, tiles * lanes), bf16),
        pltpu.VMEM((8, wide), f32),
        pltpu.VMEM((kinds * points, depth), bf16),
        pltpu.VMEM((wide, lanes), f32),
    ]
    shapes = [shape for shape in pairs for _ in range(2)]
    shapes += [pltpu.VMEM((kinds * depth, wide), f32)]
    if kinds == 3:
        shapes += [pltpu.VMEM((points, 6 * lanes), f32)] * 2 + [pltpu.VMEM((depth, 6 * lanes), bf16)]
    return shapes


def local(
    cell_points,
    cell_density,
    cell_weights,
    near_device,
    near_slot,
    near_wall,
    wall_points,
    wall_density,
    wall_weights,
):
    wall_count = lax.axis_size("wall")
    wall_index = lax.axis_index("wall")
    cells, _, points = cell_points.shape
    patch_dev, _, patch_pts = wall_points.shape
    quarter = points // wall_count
    extra = quarter - lanes
    part = patch_pts // wall_count
    vmem = pl.BlockSpec(memory_space=pltpu.VMEM)
    smem = pl.BlockSpec(memory_space=pltpu.SMEM)
    params = pltpu.CompilerParams(vmem_limit_bytes=60 * 2**20)

    cell_load = cell_density * cell_weights[:, None, :]
    raw = jnp.concatenate([2.0 * cell_points, cell_load], axis=1)
    mine = lax.dynamic_slice_in_dim(raw, wall_index * quarter, quarter, 2)
    gap = jnp.zeros((cells, lanes - 6 * extra), f32)
    ends = [mine[:, q, lanes:] for q in range(6)]
    tail = jnp.concatenate([ends[0], gap] + ends[:0:-1], axis=1)[:, None, :]
    block = jnp.concatenate([mine[:, :, :lanes], tail, jnp.zeros((cells, 1, lanes), f32)], axis=1)
    groups = lax.axis_size("cell")
    copies = jnp.broadcast_to(block[None], (groups,) + block.shape).reshape(groups * cells, 8, lanes)
    gathered = lax.all_to_all(copies, "cell", split_axis=0, concat_axis=0, tiled=True)

    wall_raw = jnp.concatenate(
        [2.0 * wall_points, wall_density * wall_weights[:, None, :], jnp.zeros((patch_dev, 2, patch_pts), f32)],
        axis=1,
    )
    wall_raw = wall_raw.reshape(patch_dev // 2, 2, 8, wall_count, part).transpose(3, 0, 2, 1, 4)
    wall_raw = wall_raw.reshape(wall_count, (patch_dev // 2) * 8, 2 * part)
    patches = exchange(wall_raw, 0).reshape(wall_count * (patch_dev // 2), 8, 2 * part)

    tiles = near_wall.shape[1] * part // lanes
    wall_term, back = pl.pallas_call(
        wall_kernel,
        out_shape=(
            jax.ShapeDtypeStruct((cells, 3, points), f32),
            jax.ShapeDtypeStruct(patches.shape, f32),
        ),
        in_specs=[smem] + [vmem] * 4,
        out_specs=(vmem, vmem),
        scratch_shapes=scratch(points, 3, tiles),
        compiler_params=params,
        cost_estimate=pl.CostEstimate(flops=7 * 10**10, bytes_accessed=10**7, transcendentals=0),
        name="wall_pairs",
    )(near_wall, patches, cell_points, cell_density, cell_weights)

    near_ids = near_device * cells + near_slot
    tiles = near_device.shape[1] + 1
    total = pl.pallas_call(
        near_kernel,
        out_shape=jax.ShapeDtypeStruct((cells, 3, points), f32),
        in_specs=[smem] + [vmem] * 5,
        out_specs=vmem,
        scratch_shapes=scratch(points, 2, tiles),
        compiler_params=params,
        cost_estimate=pl.CostEstimate(flops=7 * 10**10, bytes_accessed=10**7, transcendentals=0),
        name="near_pairs",
    )(near_ids, gathered, cell_points, cell_density, cell_weights, wall_term)

    pairs = patch_dev // 2
    total = total.reshape(cells, 3, wall_count, quarter).transpose(2, 0, 1, 3)
    back = back[:, :3, :].reshape(wall_count, pairs, 3, lanes)
    both = jnp.concatenate(
        [total.reshape(wall_count, -1, lanes), back.reshape(wall_count, -1, lanes)], axis=1
    )
    both = exchange(both, 1)
    cut = cells * 3 * quarter // lanes
    share = jnp.sum(both[:, :cut], axis=0).reshape(cells, 3, quarter)
    own = lax.dynamic_slice_in_dim(cell_density, wall_index * quarter, quarter, 2)
    velocity = 0.5 * own + two_stokes_factor * share
    back = both[:, cut:].reshape(wall_count, pairs, 3, 2, part).transpose(1, 3, 2, 0, 4)
    wall_velocity = 0.5 * wall_density + two_stokes_factor * back.reshape(patch_dev, 3, patch_pts)
    return (velocity, wall_velocity)


def solution(mesh):
    in_specs = (
        P("cell", None, None),
        P("cell", None, None),
        P("cell", None),
        P("cell", None),
        P("cell", None),
        P("cell", None),
        P(("cell", "wall"), None, None),
        P(("cell", "wall"), None, None),
        P(("cell", "wall"), None),
    )
    out_specs = (P("cell", None, "wall"), P(("cell", "wall"), None, None))
    return jax.shard_map(local, mesh=mesh, in_specs=in_specs, out_specs=out_specs, check_vma=False)
```
